32 devices in a mesh: groups: 2 (over x), space: 16 (over z, y, core).
Axes of the slice: x: 2, y: 2, z: 4, core: 2. Of those that a mesh axis runs over, the one named last changes fastest.
Arguments:
- patterns: float32 [64, 2, 128, 512], P('groups', None, 'space'), parts along dimension 0, may hold values from -8 to 8
- cases: int32 [64], P('groups'), parts along dimension 0, may hold values from 0 to 31, each once
- density: float32 [256, 512], P(('groups', 'space')), parts along dimension 0, may hold values from 0.2 to 1
- supports: int32 [256, 512], P(('groups', 'space')), parts along dimension 0, may hold values 0 or 1
Outputs:
- sensitivity: float32 [256, 512], P(('groups', 'space')), parts along dimension 0
- compliance: float32 [64], P('groups'), parts along dimension 0
The draws below stay inside these ranges and needn't reach their ends.
There are 2 independent parts, one for each index of `groups`. The reference program is written for one: setup_inputs(seed, part) draws one part's arguments, and reference() takes and returns one part's arrays. A program takes and returns all parts, laid end to end along the dimension named above; each array names one. Nothing has to cross between parts.
Inputs may be any that keep to these rules, and one draw needn't show every extreme that they name: `cases`: every pattern is used by exactly one case.
All inputs are finite; a program needn't handle non-finite values. No bound on the sum of `supports` on one device may be relied on, other than what follows from the above.
Results may differ from the reference program's by a relative error of at most 0.00015.
Values sent between devices are 32-bit elements; how exact they have to be, the bound alone decides.
No kernel may reach another device: no remote copies, remote signals or barrier semaphores. Data moves between devices by JAX's collectives and lax.ppermute only.
A program may use at most 64 MiB of HBM per device.

```python
import jax
import jax.numpy as jnp
import numpy as np
from jax import lax

NY = 512
CASES = 32
PATTERNS = 32
ITERS = 4
NX = 128


def draw_patterns(key, part):
    key = jax.random.fold_in(key, 7)
    shape = (PATTERNS, 2, NX, NY)
    height = jnp.arange(NX, dtype=jnp.float32) / NX
    rise = (0.6 + 1.4 * height)[None, None, :, None]
    values = jnp.clip(jax.random.normal(key, shape, jnp.float32), -4.0, 4.0)
    return (values * rise).astype(jnp.float32)


def plant(values, key, low, high):
    longest = values.shape.index(max(values.shape))
    spots = []
    for shift in (0, 1):
        where = [jax.random.randint(jax.random.fold_in(key, axis), (), 0, length) for axis, length in enumerate(values.shape)]
        where[longest] = (where[longest] + shift) % values.shape[longest]
        spots.append(tuple(where))
    return values.at[spots[0]].set(low).at[spots[1]].set(high)


def level_of(own_key, dims, shards, smallest, high):
    gain, own = 1.0, jax.random.fold_in(own_key, 6)
    for dim, shards_of in shards:
        draws = jnp.exp(jax.random.uniform(jax.random.fold_in(own, dim), (shards_of,), jnp.float32, smallest / len(shards), high / len(shards)))
        gain = gain * jnp.repeat(draws, dims[dim] // shards_of).reshape([-1 if axis == dim else 1 for axis in range(len(dims))])
    return gain


def setup_inputs(seed: int = 0, part: int = 0) -> dict:
    splits = jax.random.split(jax.random.key(seed), 5)
    part_splits = jax.random.split(jax.random.fold_in(splits[4], part), 5)
    patterns = draw_patterns(jax.random.fold_in(jax.random.fold_in(splits[4], part), 71), part)
    cases = jax.random.permutation(part_splits[1], CASES).astype(jnp.int32)
    density = jnp.clip(0.2 + 0.8 * jax.random.uniform(part_splits[2], (NX, NY), jnp.float32) ** level_of(part_splits[2], (NX, NY), ((0, 16),), -0.2, 0.2), 0.2, 1.0)
    supports = plant((jax.random.randint(part_splits[3], (NX, NY), 0, 16) < 1).astype(jnp.int32), jax.random.fold_in(part_splits[3], 1), 0, 1)
    return {"patterns": patterns, "cases": cases, "density": density, "supports": supports}


EMIN = 1e-3
KAPPA = 1.0
POISSON = 0.3
CENTRE = 1.5
EDGE = 0.5
CORNER = 1.5 - 2.0 ** 0.5


def element_matrix():
    nu = POISSON
    k = [0.5 - nu / 6, 0.125 + nu / 8, -0.25 - nu / 12, -0.125 + 3 * nu / 8,
         -0.25 + nu / 12, -0.125 - nu / 8, nu / 6, 0.125 - 3 * nu / 8]
    order = [[0, 1, 2, 3, 4, 5, 6, 7], [1, 0, 7, 6, 5, 4, 3, 2], [2, 7, 0, 5, 6, 3, 4, 1],
             [3, 6, 5, 0, 7, 2, 1, 4], [4, 5, 6, 7, 0, 1, 2, 3], [5, 4, 3, 2, 1, 0, 7, 6],
             [6, 3, 4, 1, 2, 7, 0, 5], [7, 2, 1, 4, 3, 6, 5, 0]]
    table = np.array([[k[j] for j in row] for row in order]) / (1 - nu ** 2)
    return jnp.array(table, dtype=jnp.float32)


def corners(padded):
    return jnp.concatenate([padded[:, :, :-1, :-1], padded[:, :, 1:, :-1],
                            padded[:, :, 1:, 1:], padded[:, :, :-1, 1:]], 0)


def assemble(forces):
    return (jnp.pad(forces[0:2], ((0, 0), (0, 0), (0, 1), (0, 1)))
            + jnp.pad(forces[2:4], ((0, 0), (0, 0), (1, 0), (0, 1)))
            + jnp.pad(forces[4:6], ((0, 0), (0, 0), (1, 0), (1, 0)))
            + jnp.pad(forces[6:8], ((0, 0), (0, 0), (0, 1), (1, 0))))


def stiff_apply(table, nodal):
    return jnp.einsum("ab,bcxy->acxy", table, nodal, precision=lax.Precision.HIGHEST)


def filter_taps(padded, rows, cols):
    taps = [[CORNER, EDGE, CORNER], [EDGE, CENTRE, EDGE], [CORNER, EDGE, CORNER]]
    total = jnp.zeros((rows, cols), jnp.float32)
    for a in range(3):
        for b in range(3):
            total = total + taps[a][b] * padded[a:a + rows, b:b + cols]
    return total


def reference(patterns, cases, density, supports):
    free = (1 - supports).astype(jnp.float32)
    fixed = supports.astype(jnp.float32)
    young = EMIN + density ** 3 * (1.0 - EMIN)
    table = element_matrix()
    onehot = (cases[:, None] == jnp.arange(PATTERNS, dtype=jnp.int32)[None, :]).astype(jnp.float32)
    force = jnp.einsum("cp,pkxy->kcxy", onehot, patterns, precision=lax.Precision.HIGHEST) * free

    def operator(field):
        masked = field * free
        padded = jnp.pad(masked, ((0, 0), (0, 0), (0, 1), (0, 1)))
        nodal = corners(padded)
        forces = young * stiff_apply(table, nodal)
        summed = assemble(forces)[:, :, :NX, :NY]
        return free * summed + fixed * field

    def inner(a, b):
        return jnp.sum(a * b, axis=(0, 2, 3))

    solution = jnp.zeros_like(force)
    residual = force
    direction = force
    norm_now = inner(residual, residual)
    for step in range(ITERS):
        image = operator(direction)
        alpha = norm_now / inner(direction, image)
        solution = solution + alpha[None, :, None, None] * direction
        residual = residual - alpha[None, :, None, None] * image
        norm_next = inner(residual, residual)
        direction = residual + (norm_next / norm_now)[None, :, None, None] * direction
        norm_now = norm_next
    padded = jnp.pad(solution, ((0, 0), (0, 0), (0, 1), (0, 1)))
    nodal = corners(padded)
    energy = jnp.sum(nodal * stiff_apply(table, nodal), axis=0)
    total = jnp.sum(young[None] * energy, axis=(1, 2))
    compliance = total / (NX * NY)
    mean = jnp.mean(total)
    weight = 1.0 / CASES + (2.0 * KAPPA / CASES) * (total - mean) / mean
    moment = -(NX * NY / mean) * 3.0 * density ** 2 * (1.0 - EMIN) * jnp.einsum(
        "c,cxy->xy", weight, energy, precision=lax.Precision.HIGHEST)
    weighted = jnp.pad(density * moment, 1)
    ones = jnp.pad(jnp.ones((NX, NY), jnp.float32), 1)
    sensitivity = filter_taps(weighted, NX, NY) / (filter_taps(ones, NX, NY) * density)
    return sensitivity, compliance
```

```python
import functools

import jax
import jax.numpy as jnp
from jax import lax
from jax.experimental import pallas as pl
from jax.experimental.pallas import tpu as pltpu
from jax.sharding import PartitionSpec as P

ITERS = 4
EMIN = 0.001
KAPPA = 1.0
NU = 0.3
CENTRE = 1.5
EDGE = 0.5
CORNER = 1.5 - 2.0**0.5

LO = ITERS
HI = ITERS + 1
MOMENTS = 2 * ITERS

STRETCH = 1.0 / (4.0 * (1.0 - NU * NU))
SHEAR = 1.0 / (8.0 * (1.0 + NU))
TWIST = (3.0 - NU) / (24.0 * (1.0 - NU * NU))

LANES = 128
SUB = 8
CHUNKS = 1


def from_next(x, lane):
    r = [pltpu.roll(p, LANES - 1, 1) for p in x]
    r.append(jnp.zeros_like(r[0]))
    return [jnp.where(lane == LANES - 1, r[c + 1], r[c]) for c in range(len(x))]


def from_prev(x, lane):
    r = [pltpu.roll(p, 1, 1) for p in x]
    r = [jnp.zeros_like(r[0])] + r
    return [jnp.where(lane == 0, r[c], r[c + 1]) for c in range(len(x))]


def pieces(row):
    return [row[..., c : c + LANES] for c in range(0, row.shape[-1], LANES)]


def mapped(f, *args):
    return [f(*a) for a in zip(*args)]


def pair_modes(x, lane):
    n = from_next(x, lane)
    return mapped(lambda a, b: a + b, x, n), mapped(lambda a, b: b - a, x, n)


def element_modes(here, above):
    (p0, m0), (p1, m1) = here, above
    gx = mapped(lambda a, b: b - a, p0, p1)
    gy = mapped(lambda a, b: b + a, m0, m1)
    tw = mapped(lambda a, b: b - a, m0, m1)
    return gx, gy, tw


def krylov_kernel(
    groups, own, lo, hi, dens, sup, *rest
):
    if len(rest) == 9:
        before, rest = rest[0], rest[1:]
    else:
        before = None
    v, msg, dext, ea, ec, eh, free, acc = rest
    rows, cols = dens.shape
    total_rows = rows + LO + HI
    lane = lax.broadcasted_iota(jnp.int32, (SUB, LANES), 1)
    sublane = lax.broadcasted_iota(jnp.int32, (SUB, LANES), 0)
    part = groups * SUB
    lo_base = part * 2 * LO
    hi_base = part * 2 * HI

    for r in range(total_rows):
        if r < LO:
            d = lo[lo_base + r : lo_base + r + 1, :]
            f = lo[lo_base + LO + r : lo_base + LO + r + 1, :]
        elif r < LO + rows:
            d = dens[r - LO : r - LO + 1, :]
            f = 1.0 - sup[r - LO : r - LO + 1, :].astype(jnp.float32)
        else:
            k = r - LO - rows
            d = hi[hi_base + k : hi_base + k + 1, :]
            f = hi[hi_base + HI + k : hi_base + HI + k + 1, :]
        free[r] = jnp.broadcast_to(f, (SUB, cols))
        dext[r : r + 1, :] = d
        if r < total_rows - 1:
            y = jnp.where(d > 0.0, EMIN + d * d * d * (1.0 - EMIN), 0.0)
            y = jnp.broadcast_to(y, (SUB, cols))
            ea[r] = y * STRETCH
            ec[r] = y * SHEAR
            eh[r] = y * TWIST

    def group(g, _):
        at = pl.ds(pl.multiple_of(g * SUB, SUB), SUB)
        for r in range(total_rows):
            for k in range(2):
                if r < LO:
                    x = lo[pl.ds(pl.multiple_of((k * LO + r) * part + g * SUB, SUB), SUB), :]
                elif r < LO + rows:
                    x = own[pl.ds(pl.multiple_of((k * rows + r - LO) * part + g * SUB, SUB), SUB), :]
                else:
                    x = hi[pl.ds(pl.multiple_of((k * HI + r - LO - rows) * part + g * SUB, SUB), SUB), :]
                v[0, k, r, at, :] = x * free[r]

        sums = [None] * MOMENTS

        def add(i, a, b):
            for p, q in zip(a, b):
                sums[i] = p * q if sums[i] is None else sums[i] + p * q

        for it in range(ITERS):
            last = it == ITERS - 1
            first_e = LO if last else it
            last_e = LO + rows - 1 if last else total_rows - 2 - it
            here = [pair_modes(pieces(v[it, k, first_e, at, :]), lane) for k in range(2)]
            prior = None
            for e in range(first_e, last_e + 1):
                above = [pair_modes(pieces(v[it, k, e + 1, at, :]), lane) for k in range(2)]
                gxu, gyu, twu = element_modes(here[0], above[0])
                gxv, gyv, twv = element_modes(here[1], above[1])
                here = above
                a, c, h = pieces(ea[e]), pieces(ec[e]), pieces(eh[e])
                tx = mapped(lambda y, s, t: y * (s + NU * t), a, gxu, gyv)
                ty = mapped(lambda y, s, t: y * (NU * s + t), a, gxu, gyv)
                gs = mapped(lambda s, t: s + t, gyu, gxv)
                tg = mapped(lambda y, s: y * s, c, gs)
                hu = mapped(lambda y, s: y * s, h, twu)
                hv = mapped(lambda y, s: y * s, h, twv)
                if last:
                    for s, t in ((tx, gxu), (ty, gyv), (tg, gs), (hu, twu), (hv, twv)):
                        add(MOMENTS - 1, s, t)
                    continue
                up = [
                    (tx, mapped(lambda s, t: s + t, tg, hu)),
                    (tg, mapped(lambda s, t: s + t, ty, hv)),
                ]
                if prior is not None:
                    dn = [mapped(lambda s, t: s - t, tg, hu), mapped(lambda s, t: s - t, ty, hv)]
                    mask = pieces(free[e])
                    for k in range(2):
                        t = mapped(lambda s, t: s - t, prior[k][0], up[k][0])
                        q = mapped(lambda s, t: s + t, prior[k][1], dn[k])
                        left = mapped(lambda s, t: s - t, t, q)
                        right = from_prev(mapped(lambda s, t: s + t, t, q), lane)
                        out = mapped(lambda s, t, m: (s + t) * m, left, right, mask)
                        for c0, o in enumerate(out):
                            v[it + 1, k, e, at, c0 * LANES : (c0 + 1) * LANES] = o
                        if LO <= e < LO + rows:
                            src = pieces(v[it, k, e, at, :])
                            if it == 0:
                                add(0, src, src)
                            add(2 * it + 1, src, out)
                            add(2 * it + 2, out, out)
                prior = up
        for i in range(MOMENTS):
            acc[i, at, :] = sums[i]
        return 0

    lax.fori_loop(0, groups, group, 0)

    for i in range(MOMENTS):
        row = jnp.zeros((SUB, LANES), jnp.float32)
        for g in range(groups):
            s = jnp.sum(acc[i, g * SUB : (g + 1) * SUB, :], axis=1, keepdims=True)
            row = row + jnp.where(lane == sublane + (g * SUB), s, 0.0)
        msg[i : i + 1, :] = jnp.sum(row, axis=0, keepdims=True)


def coefficients(m):
    zero = jnp.zeros_like(m[0])
    s_prev, s = [zero] * MOMENTS, list(m)
    a, b = [m[1] / m[0]], [m[0]]
    fine = [m[0] > 0.0]
    for k in range(1, ITERS):
        n = [None] * MOMENTS
        for l in range(k, MOMENTS - k):
            n[l] = s[l + 1] - a[k - 1] * s[l]
            if k > 1:
                n[l] = n[l] - b[k - 1] * s_prev[l]
        scale = jnp.abs(s[k + 1]) + jnp.abs(a[k - 1] * s[k])
        fine.append(fine[-1] & (n[k] > 1e-6 * scale))
        a.append(n[k + 1] / n[k] - s[k] / s[k - 1])
        b.append(n[k] / s[k - 1])
        s_prev, s = s, n
    x = [zero] * ITERS
    r = [jnp.ones_like(zero)] + [zero] * (ITERS - 1)
    p = list(r)
    total = zero
    rr, d, good = m[0], a[0], fine[0] & (a[0] > 0.0)
    for k in range(ITERS):
        alpha = jnp.where(good, 1.0 / d, 0.0)
        total = total + jnp.where(good, alpha * rr, 0.0)
        for j in range(k + 1):
            x[j] = x[j] + jnp.where(good, alpha * p[j], 0.0)
        if k + 1 < ITERS:
            r = [r[j] - (alpha * p[j - 1] if j else 0.0) for j in range(ITERS)]
            ratio = b[k + 1] / (d * d)
            p = [r[j] + ratio * p[j] for j in range(ITERS)]
            rr = rr * ratio
            d = a[k + 1] - b[k + 1] / d
            good = good & fine[k + 1] & (d > 0.0)
    return x, total


def finish_kernel(count, elements, *refs):
    vs = refs[:CHUNKS]
    msgs, dext, cases, sens, comp, energy, rimmed = refs[CHUNKS:]
    rows, cols = sens.shape
    lane = lax.broadcasted_iota(jnp.int32, (SUB, LANES), 1)
    sublane = lax.broadcasted_iota(jnp.int32, (SUB, LANES), 0)
    m = msgs[0]
    for i in range(1, msgs.shape[0]):
        m = m + msgs[i]
    xs, total = coefficients([m[i : i + 1, :] for i in range(MOMENTS)])
    real = lax.broadcasted_iota(jnp.int32, (1, LANES), 1) < count
    total = jnp.where(real, total, 0.0)
    mean = jnp.sum(total, axis=1, keepdims=True) / count
    weight = 1.0 / count + 2.0 * KAPPA / count * (total - mean) / mean

    def by_case(row, g):
        s = jnp.where(lane == sublane + g * SUB, jnp.broadcast_to(row, (SUB, LANES)), 0.0)
        return jnp.broadcast_to(jnp.sum(s, axis=1, keepdims=True), (SUB, LANES))

    picked = jnp.zeros((SUB, LANES), jnp.float32)
    for g in range(count // SUB):
        picked = picked + jnp.where(
            jnp.broadcast_to(cases[...], (SUB, LANES)) == sublane + g * SUB, by_case(total, g), 0.0
        )
    comp[...] = jnp.sum(picked, axis=0, keepdims=True) / elements

    span = rows + 2
    first = True
    for ref in vs:
        groups = ref.shape[3] // SUB
        for g in range(groups):
            gi = vs.index(ref) * groups + g
            at = slice(g * SUB, (g + 1) * SUB)
            co = [by_case(x, gi) for x in xs]
            w = by_case(weight, gi)

            def node(r):
                out = []
                for k in range(2):
                    vals = [pieces(ref[j, k, r, at, :]) for j in range(ITERS)]
                    x = mapped(lambda *q: sum(c * s for c, s in zip(co[1:], q[1:])) + co[0] * q[0], *vals)
                    out.append(pair_modes(x, lane))
                return out

            here = node(LO - 1)
            for e in range(span):
                above = node(LO + e)
                gxu, gyu, twu = element_modes(here[0], above[0])
                gxv, gyv, twv = element_modes(here[1], above[1])
                here = above
                for c in range(cols // LANES):
                    sh = gyu[c] + gxv[c]
                    en = STRETCH * (gxu[c] * gxu[c] + gyv[c] * gyv[c] + (2.0 * NU) * (gxu[c] * gyv[c]))
                    en = en + SHEAR * (sh * sh) + TWIST * (twu[c] * twu[c] + twv[c] * twv[c])
                    en = w * en
                    cs = slice(c * LANES, (c + 1) * LANES)
                    energy[e, :, cs] = en if first else energy[e, :, cs] + en
            first = False

    for e in range(span):
        d = dext[LO - 1 + e : LO + e, :]
        s = jnp.sum(energy[e], axis=0, keepdims=True)
        rimmed[e : e + 1, :] = (-(elements / mean[:, :1]) * 3.0 * (1.0 - EMIN)) * (d * d * d * s)

    def taps(get):
        up, mid, dn = get(0), get(1), get(2)
        side = mapped(lambda a, b: a + b, up, dn)
        total = mapped(lambda a, b: CENTRE * a + EDGE * b, mid, side)
        sides = mapped(lambda a, b: EDGE * a + CORNER * b, mid, side)
        left, right = from_prev(sides, lane), from_next(sides, lane)
        return mapped(lambda a, b, c: a + b + c, total, left, right)

    top = taps(lambda i: pieces(rimmed[i : i + rows, :]))
    one = taps(
        lambda i: pieces(jnp.where(dext[LO - 1 + i : LO - 1 + i + rows, :] > 0.0, 1.0, 0.0))
    )
    for c in range(cols // LANES):
        cs = slice(c * LANES, (c + 1) * LANES)
        sens[:, cs] = top[c] / (one[c] * dext[LO : LO + rows, cs])


def local(patterns, cases, density, supports):
    rows, cols = density.shape
    count = patterns.shape[0]
    tiles = lax.axis_size("space")
    part = count // CHUNKS
    groups = part // SUB
    total_rows = rows + LO + HI
    free = (1 - supports).astype(jnp.float32)
    up = [(i, i + 1) for i in range(tiles - 1)]
    down = [(i + 1, i) for i in range(tiles - 1)]

    def by_row(x):
        return jnp.transpose(x, (1, 2, 0, 3)).reshape(-1, cols)

    vmem = pl.BlockSpec(memory_space=pltpu.VMEM)

    lows, highs = [], []
    for c in range(CHUNKS):
        mine = patterns[c * part : (c + 1) * part]
        low = by_row(mine[:, :, rows - LO :])
        high = by_row(mine[:, :, :HI])
        low = jnp.concatenate([low, density[rows - LO :], free[rows - LO :]], 0)
        high = jnp.concatenate([high, density[:HI], free[:HI]], 0)
        lows.append(lax.ppermute(low, "space", up))
        highs.append(lax.ppermute(high, "space", down))

    vs = []
    for c in range(CHUNKS):
        v, msg, dext = pl.pallas_call(
            functools.partial(krylov_kernel, groups),
            out_shape=(
                jax.ShapeDtypeStruct((ITERS, 2, total_rows, part, cols), jnp.float32),
                jax.ShapeDtypeStruct((MOMENTS, LANES), jnp.float32),
                jax.ShapeDtypeStruct((total_rows, cols), jnp.float32),
            ),
            in_specs=[vmem] * 5,
            out_specs=(vmem,) * 3,
            scratch_shapes=[
                pltpu.VMEM((total_rows - 1, SUB, cols), jnp.float32),
                pltpu.VMEM((total_rows - 1, SUB, cols), jnp.float32),
                pltpu.VMEM((total_rows - 1, SUB, cols), jnp.float32),
                pltpu.VMEM((total_rows, SUB, cols), jnp.float32),
                pltpu.VMEM((MOMENTS, part, LANES), jnp.float32),
            ],
            compiler_params=pltpu.CompilerParams(vmem_limit_bytes=12 * 2**20),
            name="krylov",
        )(by_row(patterns[c * part : (c + 1) * part]), lows[c], highs[c], density, supports)
        vs.append(v)

    msgs = lax.all_to_all(jnp.broadcast_to(msg[None], (tiles,) + msg.shape), "space", 0, 0)
    padded = jnp.pad(cases, (0, LANES - count))[None]
    sens, comp = pl.pallas_call(
        functools.partial(finish_kernel, count, rows * tiles * cols),
        out_shape=(
            jax.ShapeDtypeStruct((rows, cols), jnp.float32),
            jax.ShapeDtypeStruct((1, LANES), jnp.float32),
        ),
        in_specs=[vmem] * (CHUNKS + 3),
        out_specs=(vmem,) * 2,
        scratch_shapes=[
            pltpu.VMEM((rows + 2, SUB, cols), jnp.float32),
            pltpu.VMEM((rows + SUB, cols), jnp.float32),
        ],
        compiler_params=pltpu.CompilerParams(vmem_limit_bytes=12 * 2**20),
        name="finish",
    )(*vs, msgs, dext, padded)
    return sens, comp[0, :count]


def solution(mesh):
    in_specs = (
        P("groups", None, "space", None),
        P("groups"),
        P(("groups", "space"), None),
        P(("groups", "space"), None),
    )
    out_specs = (P(("groups", "space"), None), P("groups"))
    return jax.shard_map(local, mesh=mesh, in_specs=in_specs, out_specs=out_specs, check_vma=False)
```

```python
import functools

import jax
import jax.numpy as jnp
from jax import lax
from jax.experimental import pallas as pl
from jax.experimental.pallas import tpu as pltpu
from jax.sharding import PartitionSpec as P

ITERS = 4
EMIN = 0.001
KAPPA = 1.0
NU = 0.3
CENTRE = 1.5
EDGE = 0.5
CORNER = 1.5 - 2.0**0.5

LO = ITERS
HI = ITERS + 1
MOMENTS = 2 * ITERS

STRETCH = 1.0 / (4.0 * (1.0 - NU * NU))
SHEAR = 1.0 / (8.0 * (1.0 + NU))
TWIST = (3.0 - NU) / (24.0 * (1.0 - NU * NU))

LANES = 128
SUB = 8
CHUNKS = 1


def from_next(x, lane):
    r = pltpu.roll(x[0], LANES - 1, 1)
    return x[1:] + [jnp.where(lane == LANES - 1, 0.0, r)]


def from_prev(x, lane):
    r = pltpu.roll(x[-1], 1, 1)
    return [jnp.where(lane == 0, 0.0, r)] + x[:-1]


def rearranged(x, perm):
    high = x.astype(jnp.bfloat16)
    rest = x - high.astype(jnp.float32)
    mid = rest.astype(jnp.bfloat16)
    low = (rest - mid.astype(jnp.float32)).astype(jnp.bfloat16)
    a, b, c = [jnp.dot(t, perm, preferred_element_type=jnp.float32) for t in (high, mid, low)]
    return (a + b) + c


def pieces(row):
    return [row[..., c : c + LANES] for c in range(0, row.shape[-1], LANES)]


def mapped(f, *args):
    return [f(*a) for a in zip(*args)]


def pair_modes(x, lane):
    n = from_next(x, lane)
    return mapped(lambda a, b: a + b, x, n), mapped(lambda a, b: b - a, x, n)


def element_modes(here, above):
    (p0, m0), (p1, m1) = here, above
    gx = mapped(lambda a, b: b - a, p0, p1)
    gy = mapped(lambda a, b: b + a, m0, m1)
    tw = mapped(lambda a, b: b - a, m0, m1)
    return gx, gy, tw


def pack_kernel(part, chunk, pat, dens, sup, own, lo, hi, perm, tmp):
    rows, cols = dens.shape
    width = cols // LANES
    j = lax.broadcasted_iota(jnp.int32, (cols, LANES), 0)
    l = lax.broadcasted_iota(jnp.int32, (cols, LANES), 1)
    for c in range(width):
        one = jnp.where(j == width * l + c, 1.0, 0.0).astype(jnp.bfloat16)
        perm[:, c * LANES : (c + 1) * LANES] = one
    start, size = chunk * part * 2 * rows, part * 2 * rows
    for b in range(0, size, LANES):
        y = rearranged(pat[start + b : start + b + LANES, :], perm[...])
        for c, p in enumerate(pieces(y)):
            tmp[c, b : b + LANES, :] = p
    for k in range(2):
        for r in range(rows):
            for g in range(part // SUB):
                for c in range(width):
                    x = tmp[c, pl.ds((g * SUB * 2 + k) * rows + r, SUB, stride=2 * rows), :]
                    cs = slice(c * LANES, (c + 1) * LANES)
                    at = (k * rows + r) * part + g * SUB
                    own[at : at + SUB, cs] = x
                    if r >= rows - LO:
                        at = (k * LO + r - rows + LO) * part + g * SUB
                        lo[at : at + SUB, cs] = x
                    if r < HI:
                        at = (k * HI + r) * part + g * SUB
                        hi[at : at + SUB, cs] = x
    if chunk == 0:
        both = jnp.concatenate([dens[...], 1.0 - sup[...].astype(jnp.float32)], 0)
        both = rearranged(both, perm[...])
        for i in range(2):
            field = both[i * rows : (i + 1) * rows]
            at = part * 2 * rows + i * rows
            own[at : at + rows, :] = field
            at = part * 2 * LO + i * LO
            lo[at : at + LO, :] = field[rows - LO :]
            at = part * 2 * HI + i * HI
            hi[at : at + HI, :] = field[:HI]


def krylov_kernel(groups, rows, chunk, own, lo, hi, own0, lo0, hi0, *rest):
    if chunk:
        before, rest = rest[0], rest[1:]
    v, msg, dext, ea, ec, eh, free, acc = rest
    cols = own.shape[1]
    total_rows = rows + LO + HI
    lane = lax.broadcasted_iota(jnp.int32, (SUB, LANES), 1)
    sublane = lax.broadcasted_iota(jnp.int32, (SUB, LANES), 0)
    part = groups * SUB
    lo_base, own_base, hi_base = part * 2 * LO, part * 2 * rows, part * 2 * HI

    for r in range(total_rows):
        if r < LO:
            d = lo0[lo_base + r : lo_base + r + 1, :]
            f = lo0[lo_base + LO + r : lo_base + LO + r + 1, :]
        elif r < LO + rows:
            k = own_base + r - LO
            d = own0[k : k + 1, :]
            f = own0[k + rows : k + rows + 1, :]
        else:
            k = r - LO - rows
            d = hi0[hi_base + k : hi_base + k + 1, :]
            f = hi0[hi_base + HI + k : hi_base + HI + k + 1, :]
        free[r] = jnp.broadcast_to(f, (SUB, cols))
        dext[r : r + 1, :] = d
        if r < total_rows - 1:
            y = jnp.where(d > 0.0, EMIN + d * d * d * (1.0 - EMIN), 0.0)
            y = jnp.broadcast_to(y, (SUB, cols))
            ea[r] = y * STRETCH
            ec[r] = y * SHEAR
            eh[r] = y * TWIST

    def group(g, _):
        at = pl.ds(pl.multiple_of(g * SUB, SUB), SUB)
        for r in range(total_rows):
            for k in range(2):
                if r < LO:
                    x = lo[pl.ds(pl.multiple_of((k * LO + r) * part + g * SUB, SUB), SUB), :]
                elif r < LO + rows:
                    x = own[pl.ds(pl.multiple_of((k * rows + r - LO) * part + g * SUB, SUB), SUB), :]
                else:
                    x = hi[pl.ds(pl.multiple_of((k * HI + r - LO - rows) * part + g * SUB, SUB), SUB), :]
                v[0, k, r, at, :] = x * free[r]

        sums = [None] * MOMENTS

        def add(i, a, b):
            for p, q in zip(a, b):
                sums[i] = p * q if sums[i] is None else sums[i] + p * q

        for it in range(ITERS):
            last = it == ITERS - 1
            first_e = LO if last else it
            last_e = LO + rows - 1 if last else total_rows - 2 - it
            here = [pair_modes(pieces(v[it, k, first_e, at, :]), lane) for k in range(2)]
            prior = None
            for e in range(first_e, last_e + 1):
                above = [pair_modes(pieces(v[it, k, e + 1, at, :]), lane) for k in range(2)]
                gxu, gyu, twu = element_modes(here[0], above[0])
                gxv, gyv, twv = element_modes(here[1], above[1])
                here = above
                a, c, h = pieces(ea[e]), pieces(ec[e]), pieces(eh[e])
                tx = mapped(lambda y, s, t: y * (s + NU * t), a, gxu, gyv)
                ty = mapped(lambda y, s, t: y * (NU * s + t), a, gxu, gyv)
                gs = mapped(lambda s, t: s + t, gyu, gxv)
                tg = mapped(lambda y, s: y * s, c, gs)
                hu = mapped(lambda y, s: y * s, h, twu)
                hv = mapped(lambda y, s: y * s, h, twv)
                if last:
                    for s, t in ((tx, gxu), (ty, gyv), (tg, gs), (hu, twu), (hv, twv)):
                        add(MOMENTS - 1, s, t)
                    continue
                up = [
                    (tx, mapped(lambda s, t: s + t, tg, hu)),
                    (tg, mapped(lambda s, t: s + t, ty, hv)),
                ]
                if prior is not None:
                    dn = [mapped(lambda s, t: s - t, tg, hu), mapped(lambda s, t: s - t, ty, hv)]
                    mask = pieces(free[e])
                    for k in range(2):
                        t = mapped(lambda s, t: s - t, prior[k][0], up[k][0])
                        q = mapped(lambda s, t: s + t, prior[k][1], dn[k])
                        left = mapped(lambda s, t: s - t, t, q)
                        right = from_prev(mapped(lambda s, t: s + t, t, q), lane)
                        out = mapped(lambda s, t, m: (s + t) * m, left, right, mask)
                        for c0, o in enumerate(out):
                            v[it + 1, k, e, at, c0 * LANES : (c0 + 1) * LANES] = o
                        if LO <= e < LO + rows:
                            src = pieces(v[it, k, e, at, :])
                            if it == 0:
                                add(0, src, src)
                            add(2 * it + 1, src, out)
                            add(2 * it + 2, out, out)
                prior = up
        for i in range(MOMENTS):
            acc[i, at, :] = sums[i]
        return 0

    lax.fori_loop(0, groups, group, 0)

    for i in range(MOMENTS):
        row = jnp.zeros((SUB, LANES), jnp.float32)
        for g in range(groups):
            s = jnp.sum(acc[i, g * SUB : (g + 1) * SUB, :], axis=1, keepdims=True)
            row = row + jnp.where(lane == sublane + (chunk * part + g * SUB), s, 0.0)
        row = jnp.sum(row, axis=0, keepdims=True)
        msg[i : i + 1, :] = row + before[i : i + 1, :] if chunk else row


def coefficients(m):
    zero = jnp.zeros_like(m[0])
    s_prev, s = [zero] * MOMENTS, list(m)
    a, b = [m[1] / m[0]], [m[0]]
    fine = [m[0] > 0.0]
    for k in range(1, ITERS):
        n = [None] * MOMENTS
        for l in range(k, MOMENTS - k):
            n[l] = s[l + 1] - a[k - 1] * s[l]
            if k > 1:
                n[l] = n[l] - b[k - 1] * s_prev[l]
        scale = jnp.abs(s[k + 1]) + jnp.abs(a[k - 1] * s[k])
        fine.append(fine[-1] & (n[k] > 1e-6 * scale))
        a.append(n[k + 1] / n[k] - s[k] / s[k - 1])
        b.append(n[k] / s[k - 1])
        s_prev, s = s, n
    x = [zero] * ITERS
    r = [jnp.ones_like(zero)] + [zero] * (ITERS - 1)
    p = list(r)
    total = zero
    rr, d, good = m[0], a[0], fine[0] & (a[0] > 0.0)
    for k in range(ITERS):
        alpha = jnp.where(good, 1.0 / d, 0.0)
        total = total + jnp.where(good, alpha * rr, 0.0)
        for j in range(k + 1):
            x[j] = x[j] + jnp.where(good, alpha * p[j], 0.0)
        if k + 1 < ITERS:
            r = [r[j] - (alpha * p[j - 1] if j else 0.0) for j in range(ITERS)]
            ratio = b[k + 1] / (d * d)
            p = [r[j] + ratio * p[j] for j in range(ITERS)]
            rr = rr * ratio
            d = a[k + 1] - b[k + 1] / d
            good = good & fine[k + 1] & (d > 0.0)
    return x, total


def finish_kernel(count, elements, *refs):
    vs = refs[:CHUNKS]
    msgs, dext, cases, sens, comp, energy, rimmed, perm = refs[CHUNKS:]
    rows, cols = sens.shape
    lane = lax.broadcasted_iota(jnp.int32, (SUB, LANES), 1)
    sublane = lax.broadcasted_iota(jnp.int32, (SUB, LANES), 0)
    m = msgs[0]
    for i in range(1, msgs.shape[0]):
        m = m + msgs[i]
    xs, total = coefficients([m[i : i + 1, :] for i in range(MOMENTS)])
    real = lax.broadcasted_iota(jnp.int32, (1, LANES), 1) < count
    total = jnp.where(real, total, 0.0)
    mean = jnp.sum(total, axis=1, keepdims=True) / count
    weight = 1.0 / count + 2.0 * KAPPA / count * (total - mean) / mean

    def by_case(row, g):
        s = jnp.where(lane == sublane + g * SUB, jnp.broadcast_to(row, (SUB, LANES)), 0.0)
        return jnp.broadcast_to(jnp.sum(s, axis=1, keepdims=True), (SUB, LANES))

    picked = jnp.zeros((SUB, count), jnp.float32)
    for g in range(count // SUB):
        match = jnp.broadcast_to(cases[...], (SUB, count)) == sublane[:, :count] + g * SUB
        picked = picked + jnp.where(match, by_case(total, g)[:, :count], 0.0)
    comp[...] = jnp.sum(picked, axis=0, keepdims=True) / elements

    span = rows + 2
    first = True
    for ref in vs:
        groups = ref.shape[3] // SUB
        for g in range(groups):
            gi = vs.index(ref) * groups + g
            at = slice(g * SUB, (g + 1) * SUB)
            co = [by_case(x, gi) for x in xs]
            w = by_case(weight, gi)

            def node(r):
                out = []
                for k in range(2):
                    vals = [pieces(ref[j, k, r, at, :]) for j in range(ITERS)]
                    x = mapped(lambda *q: sum(c * s for c, s in zip(co[1:], q[1:])) + co[0] * q[0], *vals)
                    out.append(pair_modes(x, lane))
                return out

            here = node(LO - 1)
            for e in range(span):
                above = node(LO + e)
                gxu, gyu, twu = element_modes(here[0], above[0])
                gxv, gyv, twv = element_modes(here[1], above[1])
                here = above
                for c in range(cols // LANES):
                    sh = gyu[c] + gxv[c]
                    en = STRETCH * (gxu[c] * gxu[c] + gyv[c] * gyv[c] + (2.0 * NU) * (gxu[c] * gyv[c]))
                    en = en + SHEAR * (sh * sh) + TWIST * (twu[c] * twu[c] + twv[c] * twv[c])
                    en = w * en
                    cs = slice(c * LANES, (c + 1) * LANES)
                    energy[e, :, cs] = en if first else energy[e, :, cs] + en
            first = False

    for e in range(span):
        d = dext[LO - 1 + e : LO + e, :]
        s = jnp.sum(energy[e], axis=0, keepdims=True)
        rimmed[e : e + 1, :] = (-(elements / mean[:, :1]) * 3.0 * (1.0 - EMIN)) * (d * d * d * s)

    def taps(get):
        up, mid, dn = get(0), get(1), get(2)
        side = mapped(lambda a, b: a + b, up, dn)
        total = mapped(lambda a, b: CENTRE * a + EDGE * b, mid, side)
        sides = mapped(lambda a, b: EDGE * a + CORNER * b, mid, side)
        left, right = from_prev(sides, lane), from_next(sides, lane)
        return mapped(lambda a, b, c: a + b + c, total, left, right)

    width = cols // LANES
    i = lax.broadcasted_iota(jnp.int32, (LANES, cols), 0)
    j = lax.broadcasted_iota(jnp.int32, (LANES, cols), 1)
    for c in range(width):
        one = jnp.where(j == width * i + c, 1.0, 0.0).astype(jnp.bfloat16)
        perm[c * LANES : (c + 1) * LANES, :] = one

    top = taps(lambda i: pieces(rimmed[i : i + rows, :]))
    one = taps(
        lambda i: pieces(jnp.where(dext[LO - 1 + i : LO - 1 + i + rows, :] > 0.0, 1.0, 0.0))
    )
    own = pieces(dext[LO : LO + rows, :])
    out = jnp.concatenate([t / (o * d) for t, o, d in zip(top, one, own)], 1)
    sens[...] = rearranged(out, perm[...])


def local(patterns, cases, density, supports):
    rows, cols = density.shape
    count = patterns.shape[0]
    tiles = lax.axis_size("space")
    part = count // CHUNKS
    groups = part // SUB
    total_rows = rows + LO + HI
    up = [(i, i + 1) for i in range(tiles - 1)]
    down = [(i + 1, i) for i in range(tiles - 1)]
    flat = patterns.reshape(count * 2 * rows, cols)
    vmem = pl.BlockSpec(memory_space=pltpu.VMEM)
    params = pltpu.CompilerParams(vmem_limit_bytes=12 * 2**20)

    def shape(*dims):
        return jax.ShapeDtypeStruct(dims, jnp.float32)

    owns, lows, highs = [], [], []
    for c in range(CHUNKS):
        extra = 0 if c else 2
        own, low, high = pl.pallas_call(
            functools.partial(pack_kernel, part, c),
            out_shape=tuple(shape(n * (2 * part + extra), cols) for n in (rows, LO, HI)),
            in_specs=[vmem] * 3,
            out_specs=(vmem,) * 3,
            scratch_shapes=[
                pltpu.VMEM((cols, cols), jnp.bfloat16),
                pltpu.VMEM((cols // LANES, part * 2 * rows, LANES), jnp.float32),
            ],
            compiler_params=params,
            name="pack",
        )(flat, density, supports)
        owns.append(own)
        lows.append(lax.ppermute(low, "space", up))
        highs.append(lax.ppermute(high, "space", down))

    vs, msg = [], None
    for c in range(CHUNKS):
        args = (owns[c], lows[c], highs[c], owns[0], lows[0], highs[0]) + ((msg,) if c else ())
        v, msg, dext = pl.pallas_call(
            functools.partial(krylov_kernel, groups, rows, c),
            out_shape=(
                shape(ITERS, 2, total_rows, part, cols),
                shape(MOMENTS, LANES),
                shape(total_rows, cols),
            ),
            in_specs=[vmem] * len(args),
            out_specs=(vmem,) * 3,
            scratch_shapes=[
                pltpu.VMEM((total_rows - 1, SUB, cols), jnp.float32),
                pltpu.VMEM((total_rows - 1, SUB, cols), jnp.float32),
                pltpu.VMEM((total_rows - 1, SUB, cols), jnp.float32),
                pltpu.VMEM((total_rows, SUB, cols), jnp.float32),
                pltpu.VMEM((MOMENTS, part, LANES), jnp.float32),
            ],
            compiler_params=params,
            name="krylov",
        )(*args)
        vs.append(v)

    b = 1
    while b < tiles:
        msg = msg + lax.ppermute(msg, "space", [(i, i ^ b) for i in range(tiles)])
        b *= 2
    msgs = msg[None]
    sens, comp = pl.pallas_call(
        functools.partial(finish_kernel, count, rows * tiles * cols),
        out_shape=(shape(rows, cols), shape(1, count)),
        in_specs=[vmem] * (CHUNKS + 3),
        out_specs=(vmem,) * 2,
        scratch_shapes=[
            pltpu.VMEM((rows + 2, SUB, cols), jnp.float32),
            pltpu.VMEM((rows + SUB, cols), jnp.float32),
            pltpu.VMEM((cols, cols), jnp.bfloat16),
        ],
        compiler_params=params,
        name="finish",
    )(*vs, msgs, dext, cases[None])
    return sens, comp.reshape(count)


def solution(mesh):
    in_specs = (
        P("groups", None, "space", None),
        P("groups"),
        P(("groups", "space"), None),
        P(("groups", "space"), None),
    )
    out_specs = (P(("groups", "space"), None), P("groups"))
    return jax.shard_map(local, mesh=mesh, in_specs=in_specs, out_specs=out_specs, check_vma=False)
```

```python
import functools

import jax
import jax.numpy as jnp
from jax import lax
from jax.experimental import pallas as pl
from jax.experimental.pallas import tpu as pltpu
from jax.sharding import PartitionSpec as P

ITERS = 4
EMIN = 0.001
KAPPA = 1.0
NU = 0.3
CENTRE = 1.5
EDGE = 0.5
CORNER = 1.5 - 2.0**0.5

LO = ITERS
HI = ITERS + 1
MOMENTS = 2 * ITERS

STRETCH = 1.0 / (4.0 * (1.0 - NU * NU))
SHEAR = 1.0 / (8.0 * (1.0 + NU))
TWIST = (3.0 - NU) / (24.0 * (1.0 - NU * NU))

LANES = 128
SUB = 8
SHARES = 2


def from_next(x, lane):
    r = pltpu.roll(x[0], LANES - 1, 1)
    return x[1:] + [jnp.where(lane == LANES - 1, 0.0, r)]


def from_prev(x, lane):
    r = pltpu.roll(x[-1], 1, 1)
    return [jnp.where(lane == 0, 0.0, r)] + x[:-1]


def rearranged(x, perm):
    high = x.astype(jnp.bfloat16)
    rest = x - high.astype(jnp.float32)
    mid = rest.astype(jnp.bfloat16)
    low = (rest - mid.astype(jnp.float32)).astype(jnp.bfloat16)
    a, b, c = [jnp.dot(t, perm, preferred_element_type=jnp.float32) for t in (high, mid, low)]
    return (a + b) + c


def pieces(row):
    return [row[..., c : c + LANES] for c in range(0, row.shape[-1], LANES)]


def mapped(f, *args):
    return [f(*a) for a in zip(*args)]


def pair_modes(x, lane):
    n = from_next(x, lane)
    return mapped(lambda a, b: a + b, x, n), mapped(lambda a, b: b - a, x, n)


def element_modes(here, above):
    (p0, m0), (p1, m1) = here, above
    gx = mapped(lambda a, b: b - a, p0, p1)
    gy = mapped(lambda a, b: b + a, m0, m1)
    tw = mapped(lambda a, b: b - a, m0, m1)
    return gx, gy, tw


def pack_kernel(part, base, pat, dens, sup, own, lo, hi, perm, tmp):
    rows, cols = dens.shape
    width = cols // LANES
    j = lax.broadcasted_iota(jnp.int32, (cols, LANES), 0)
    l = lax.broadcasted_iota(jnp.int32, (cols, LANES), 1)
    for c in range(width):
        one = jnp.where(j == width * l + c, 1.0, 0.0).astype(jnp.bfloat16)
        perm[:, c * LANES : (c + 1) * LANES] = one
    start, size = base * 2 * rows, part * 2 * rows
    for b in range(0, size, LANES):
        y = rearranged(pat[start + b : start + b + LANES, :], perm[...])
        for c, p in enumerate(pieces(y)):
            tmp[c, b : b + LANES, :] = p
    for k in range(2):
        for r in range(rows):
            for g in range(part // SUB):
                for c in range(width):
                    x = tmp[c, pl.ds((g * SUB * 2 + k) * rows + r, SUB, stride=2 * rows), :]
                    cs = slice(c * LANES, (c + 1) * LANES)
                    at = (k * rows + r) * part + g * SUB
                    own[at : at + SUB, cs] = x
                    if r >= rows - LO:
                        at = (k * LO + r - rows + LO) * part + g * SUB
                        lo[at : at + SUB, cs] = x
                    if r < HI:
                        at = (k * HI + r) * part + g * SUB
                        hi[at : at + SUB, cs] = x
    if base == 0:
        both = jnp.concatenate([dens[...], 1.0 - sup[...].astype(jnp.float32)], 0)
        both = rearranged(both, perm[...])
        for i in range(2):
            field = both[i * rows : (i + 1) * rows]
            at = part * 2 * rows + i * rows
            own[at : at + rows, :] = field
            at = part * 2 * LO + i * LO
            lo[at : at + LO, :] = field[rows - LO :]
            at = part * 2 * HI + i * HI
            hi[at : at + HI, :] = field[:HI]


def krylov_kernel(groups, rows, base, own, lo, hi, own0, lo0, hi0, *rest):
    if base:
        before, rest = rest[0], rest[1:]
    v, msg, dext, ea, ec, eh, free, acc = rest
    cols = own.shape[1]
    total_rows = rows + LO + HI
    lane = lax.broadcasted_iota(jnp.int32, (SUB, LANES), 1)
    sublane = lax.broadcasted_iota(jnp.int32, (SUB, LANES), 0)
    part = groups * SUB
    lo_base, own_base = lo0.shape[0] - 2 * LO, own0.shape[0] - 2 * rows
    hi_base = hi0.shape[0] - 2 * HI

    for r in range(total_rows):
        if r < LO:
            d = lo0[lo_base + r : lo_base + r + 1, :]
            f = lo0[lo_base + LO + r : lo_base + LO + r + 1, :]
        elif r < LO + rows:
            k = own_base + r - LO
            d = own0[k : k + 1, :]
            f = own0[k + rows : k + rows + 1, :]
        else:
            k = r - LO - rows
            d = hi0[hi_base + k : hi_base + k + 1, :]
            f = hi0[hi_base + HI + k : hi_base + HI + k + 1, :]
        free[r] = jnp.broadcast_to(f, (SUB, cols))
        dext[r : r + 1, :] = d
        if r < total_rows - 1:
            y = jnp.where(d > 0.0, EMIN + d * d * d * (1.0 - EMIN), 0.0)
            y = jnp.broadcast_to(y, (SUB, cols))
            ea[r] = y * STRETCH
            ec[r] = y * SHEAR
            eh[r] = y * TWIST

    def group(g, _):
        at = pl.ds(pl.multiple_of(g * SUB, SUB), SUB)
        for r in range(total_rows):
            for k in range(2):
                if r < LO:
                    x = lo[pl.ds(pl.multiple_of((k * LO + r) * part + g * SUB, SUB), SUB), :]
                elif r < LO + rows:
                    x = own[pl.ds(pl.multiple_of((k * rows + r - LO) * part + g * SUB, SUB), SUB), :]
                else:
                    x = hi[pl.ds(pl.multiple_of((k * HI + r - LO - rows) * part + g * SUB, SUB), SUB), :]
                v[0, k, r, at, :] = x * free[r]

        sums = [None] * MOMENTS

        def add(i, a, b):
            for p, q in zip(a, b):
                sums[i] = p * q if sums[i] is None else sums[i] + p * q

        for it in range(ITERS):
            last = it == ITERS - 1
            first_e = LO if last else it
            last_e = LO + rows - 1 if last else total_rows - 2 - it
            here = [pair_modes(pieces(v[it, k, first_e, at, :]), lane) for k in range(2)]
            prior = None
            for e in range(first_e, last_e + 1):
                above = [pair_modes(pieces(v[it, k, e + 1, at, :]), lane) for k in range(2)]
                gxu, gyu, twu = element_modes(here[0], above[0])
                gxv, gyv, twv = element_modes(here[1], above[1])
                here = above
                a, c, h = pieces(ea[e]), pieces(ec[e]), pieces(eh[e])
                tx = mapped(lambda y, s, t: y * (s + NU * t), a, gxu, gyv)
                ty = mapped(lambda y, s, t: y * (NU * s + t), a, gxu, gyv)
                gs = mapped(lambda s, t: s + t, gyu, gxv)
                tg = mapped(lambda y, s: y * s, c, gs)
                hu = mapped(lambda y, s: y * s, h, twu)
                hv = mapped(lambda y, s: y * s, h, twv)
                if last:
                    for s, t in ((tx, gxu), (ty, gyv), (tg, gs), (hu, twu), (hv, twv)):
                        add(MOMENTS - 1, s, t)
                    continue
                up = [
                    (tx, mapped(lambda s, t: s + t, tg, hu)),
                    (tg, mapped(lambda s, t: s + t, ty, hv)),
                ]
                if prior is not None:
                    dn = [mapped(lambda s, t: s - t, tg, hu), mapped(lambda s, t: s - t, ty, hv)]
                    mask = pieces(free[e])
                    for k in range(2):
                        t = mapped(lambda s, t: s - t, prior[k][0], up[k][0])
                        q = mapped(lambda s, t: s + t, prior[k][1], dn[k])
                        left = mapped(lambda s, t: s - t, t, q)
                        right = from_prev(mapped(lambda s, t: s + t, t, q), lane)
                        out = mapped(lambda s, t, m: (s + t) * m, left, right, mask)
                        for c0, o in enumerate(out):
                            v[it + 1, k, e, at, c0 * LANES : (c0 + 1) * LANES] = o
                        if LO <= e < LO + rows:
                            src = pieces(v[it, k, e, at, :])
                            if it == 0:
                                add(0, src, src)
                            add(2 * it + 1, src, out)
                            add(2 * it + 2, out, out)
                prior = up
        for i in range(MOMENTS):
            acc[i, at, :] = sums[i]
        return 0

    lax.fori_loop(0, groups, group, 0)

    for i in range(MOMENTS):
        row = jnp.zeros((SUB, LANES), jnp.float32)
        for g in range(groups):
            s = jnp.sum(acc[i, g * SUB : (g + 1) * SUB, :], axis=1, keepdims=True)
            row = row + jnp.where(lane == sublane + (base + g * SUB), s, 0.0)
        row = jnp.sum(row, axis=0, keepdims=True)
        row = row + before[0, i : i + 1, :] if base else row
        for t in range(msg.shape[0]):
            msg[t, i : i + 1, :] = row


def coefficients(m):
    zero = jnp.zeros_like(m[0])
    s_prev, s = [zero] * MOMENTS, list(m)
    a, b = [m[1] / m[0]], [m[0]]
    fine = [m[0] > 0.0]
    for k in range(1, ITERS):
        n = [None] * MOMENTS
        for l in range(k, MOMENTS - k):
            n[l] = s[l + 1] - a[k - 1] * s[l]
            if k > 1:
                n[l] = n[l] - b[k - 1] * s_prev[l]
        scale = jnp.abs(s[k + 1]) + jnp.abs(a[k - 1] * s[k])
        fine.append(fine[-1] & (n[k] > 1e-6 * scale))
        a.append(n[k + 1] / n[k] - s[k] / s[k - 1])
        b.append(n[k] / s[k - 1])
        s_prev, s = s, n
    x = [zero] * ITERS
    r = [jnp.ones_like(zero)] + [zero] * (ITERS - 1)
    p = list(r)
    total = zero
    rr, d, good = m[0], a[0], fine[0] & (a[0] > 0.0)
    for k in range(ITERS):
        alpha = jnp.where(good, 1.0 / d, 0.0)
        total = total + jnp.where(good, alpha * rr, 0.0)
        for j in range(k + 1):
            x[j] = x[j] + jnp.where(good, alpha * p[j], 0.0)
        if k + 1 < ITERS:
            r = [r[j] - (alpha * p[j - 1] if j else 0.0) for j in range(ITERS)]
            ratio = b[k + 1] / (d * d)
            p = [r[j] + ratio * p[j] for j in range(ITERS)]
            rr = rr * ratio
            d = a[k + 1] - b[k + 1] / d
            good = good & fine[k + 1] & (d > 0.0)
    return x, total


def finish_kernel(count, elements, *refs):
    vs, refs = refs[:-8], refs[-8:]
    msgs, dext, cases, sens, comp, energy, rimmed, perm = refs
    rows, cols = sens.shape
    lane = lax.broadcasted_iota(jnp.int32, (SUB, LANES), 1)
    sublane = lax.broadcasted_iota(jnp.int32, (SUB, LANES), 0)
    m = msgs[0]
    for i in range(1, msgs.shape[0]):
        m = m + msgs[i]
    xs, total = coefficients([m[i : i + 1, :] for i in range(MOMENTS)])
    real = lax.broadcasted_iota(jnp.int32, (1, LANES), 1) < count
    total = jnp.where(real, total, 0.0)
    mean = jnp.sum(total, axis=1, keepdims=True) / count
    weight = 1.0 / count + 2.0 * KAPPA / count * (total - mean) / mean

    def by_case(row, g):
        s = jnp.where(lane == sublane + g * SUB, jnp.broadcast_to(row, (SUB, LANES)), 0.0)
        return jnp.broadcast_to(jnp.sum(s, axis=1, keepdims=True), (SUB, LANES))

    picked = jnp.zeros((SUB, count), jnp.float32)
    for g in range(count // SUB):
        match = jnp.broadcast_to(cases[...], (SUB, count)) == sublane[:, :count] + g * SUB
        picked = picked + jnp.where(match, by_case(total, g)[:, :count], 0.0)
    comp[...] = jnp.sum(picked, axis=0, keepdims=True) / elements

    span = rows + 2
    first = True
    gi = -1
    for ref in vs:
        groups = ref.shape[3] // SUB
        for g in range(groups):
            gi += 1
            at = slice(g * SUB, (g + 1) * SUB)
            co = [by_case(x, gi) for x in xs]
            w = by_case(weight, gi)

            def node(r):
                out = []
                for k in range(2):
                    vals = [pieces(ref[j, k, r, at, :]) for j in range(ITERS)]
                    x = mapped(lambda *q: sum(c * s for c, s in zip(co[1:], q[1:])) + co[0] * q[0], *vals)
                    out.append(pair_modes(x, lane))
                return out

            here = node(LO - 1)
            for e in range(span):
                above = node(LO + e)
                gxu, gyu, twu = element_modes(here[0], above[0])
                gxv, gyv, twv = element_modes(here[1], above[1])
                here = above
                for c in range(cols // LANES):
                    sh = gyu[c] + gxv[c]
                    en = STRETCH * (gxu[c] * gxu[c] + gyv[c] * gyv[c] + (2.0 * NU) * (gxu[c] * gyv[c]))
                    en = en + SHEAR * (sh * sh) + TWIST * (twu[c] * twu[c] + twv[c] * twv[c])
                    en = w * en
                    cs = slice(c * LANES, (c + 1) * LANES)
                    energy[e, :, cs] = en if first else energy[e, :, cs] + en
            first = False

    for e in range(span):
        d = dext[LO - 1 + e : LO + e, :]
        s = jnp.sum(energy[e], axis=0, keepdims=True)
        rimmed[e : e + 1, :] = (-(elements / mean[:, :1]) * 3.0 * (1.0 - EMIN)) * (d * d * d * s)

    def taps(get):
        up, mid, dn = get(0), get(1), get(2)
        side = mapped(lambda a, b: a + b, up, dn)
        total = mapped(lambda a, b: CENTRE * a + EDGE * b, mid, side)
        sides = mapped(lambda a, b: EDGE * a + CORNER * b, mid, side)
        left, right = from_prev(sides, lane), from_next(sides, lane)
        return mapped(lambda a, b, c: a + b + c, total, left, right)

    width = cols // LANES
    i = lax.broadcasted_iota(jnp.int32, (LANES, cols), 0)
    j = lax.broadcasted_iota(jnp.int32, (LANES, cols), 1)
    for c in range(width):
        one = jnp.where(j == width * i + c, 1.0, 0.0).astype(jnp.bfloat16)
        perm[c * LANES : (c + 1) * LANES, :] = one

    top = taps(lambda i: pieces(rimmed[i : i + rows, :]))
    one = taps(
        lambda i: pieces(jnp.where(dext[LO - 1 + i : LO - 1 + i + rows, :] > 0.0, 1.0, 0.0))
    )
    own = pieces(dext[LO : LO + rows, :])
    out = jnp.concatenate([t / (o * d) for t, o, d in zip(top, one, own)], 1)
    sens[...] = rearranged(out, perm[...])


def local(patterns, cases, density, supports):
    rows, cols = density.shape
    count = patterns.shape[0]
    tiles = lax.axis_size("space")
    parts = [count // SHARES] * SHARES
    total_rows = rows + LO + HI
    up = [(i, i + 1) for i in range(tiles - 1)]
    down = [(i + 1, i) for i in range(tiles - 1)]
    flat = patterns.reshape(count * 2 * rows, cols)
    vmem = pl.BlockSpec(memory_space=pltpu.VMEM)
    params = pltpu.CompilerParams(vmem_limit_bytes=12 * 2**20)

    def shape(*dims):
        return jax.ShapeDtypeStruct(dims, jnp.float32)

    owns, lows, highs = [], [], []
    for c, part in enumerate(parts):
        base = sum(parts[:c])
        extra = 0 if c else 2
        own, low, high = pl.pallas_call(
            functools.partial(pack_kernel, part, base),
            out_shape=tuple(shape(n * (2 * part + extra), cols) for n in (rows, LO, HI)),
            in_specs=[vmem] * 3,
            out_specs=(vmem,) * 3,
            scratch_shapes=[
                pltpu.VMEM((cols, cols), jnp.bfloat16),
                pltpu.VMEM((cols // LANES, part * 2 * rows, LANES), jnp.float32),
            ],
            compiler_params=params,
            name="pack",
        )(flat, density, supports)
        owns.append(own)
        lows.append(lax.ppermute(low, "space", up))
        highs.append(lax.ppermute(high, "space", down))

    vs, msg = [], None
    for c, part in enumerate(parts):
        args = (owns[c], lows[c], highs[c], owns[0], lows[0], highs[0]) + ((msg,) if c else ())
        v, msg, dext = pl.pallas_call(
            functools.partial(krylov_kernel, part // SUB, rows, sum(parts[:c])),
            out_shape=(
                shape(ITERS, 2, total_rows, part, cols),
                shape(tiles if c + 1 == len(parts) else 1, MOMENTS, LANES),
                shape(total_rows, cols),
            ),
            in_specs=[vmem] * len(args),
            out_specs=(vmem,) * 3,
            scratch_shapes=[
                pltpu.VMEM((total_rows - 1, SUB, cols), jnp.float32),
                pltpu.VMEM((total_rows - 1, SUB, cols), jnp.float32),
                pltpu.VMEM((total_rows - 1, SUB, cols), jnp.float32),
                pltpu.VMEM((total_rows, SUB, cols), jnp.float32),
                pltpu.VMEM((MOMENTS, part, LANES), jnp.float32),
            ],
            compiler_params=params,
            cost_estimate=pl.CostEstimate(flops=10**10, bytes_accessed=40 * 10**6, transcendentals=0),
            name="krylov",
        )(*args)
        vs.append(v)

    msgs = lax.all_to_all(msg, "space", 0, 0)
    sens, comp = pl.pallas_call(
        functools.partial(finish_kernel, count, rows * tiles * cols),
        out_shape=(shape(rows, cols), shape(1, count)),
        in_specs=[vmem] * (len(vs) + 3),
        out_specs=(vmem,) * 2,
        scratch_shapes=[
            pltpu.VMEM((rows + 2, SUB, cols), jnp.float32),
            pltpu.VMEM((rows + SUB, cols), jnp.float32),
            pltpu.VMEM((cols, cols), jnp.bfloat16),
        ],
        compiler_params=params,
        name="finish",
    )(*vs, msgs, dext, cases[None])
    return sens, comp.reshape(count)


def solution(mesh):
    in_specs = (
        P("groups", None, "space", None),
        P("groups"),
        P(("groups", "space"), None),
        P(("groups", "space"), None),
    )
    out_specs = (P(("groups", "space"), None), P("groups"))
    return jax.shard_map(local, mesh=mesh, in_specs=in_specs, out_specs=out_specs, check_vma=False)
```

```python
import functools

import jax
import jax.numpy as jnp
from jax import lax
from jax.experimental import pallas as pl
from jax.experimental.pallas import tpu as pltpu
from jax.sharding import PartitionSpec as P

ITERS = 4
EMIN = 0.001
KAPPA = 1.0
NU = 0.3
CENTRE = 1.5
EDGE = 0.5
CORNER = 1.5 - 2.0**0.5

LO = ITERS
HI = ITERS + 1
MOMENTS = 2 * ITERS

STRETCH = 1.0 / (4.0 * (1.0 - NU * NU))
SHEAR = 1.0 / (8.0 * (1.0 + NU))
TWIST = (3.0 - NU) / (24.0 * (1.0 - NU * NU))

LANES = 128
SUB = 8
SHARES = 2


def from_next(x, lane):
    r = pltpu.roll(x[0], LANES - 1, 1)
    return x[1:] + [jnp.where(lane == LANES - 1, 0.0, r)]


def from_prev(x, lane):
    r = pltpu.roll(x[-1], 1, 1)
    return [jnp.where(lane == 0, 0.0, r)] + x[:-1]


def taps(lane, up, mid, dn):
    side = mapped(lambda a, b: a + b, up, dn)
    total = mapped(lambda a, b: CENTRE * a + EDGE * b, mid, side)
    sides = mapped(lambda a, b: EDGE * a + CORNER * b, mid, side)
    left, right = from_prev(sides, lane), from_next(sides, lane)
    return mapped(lambda a, b, c: a + b + c, total, left, right)


def rearranged(x, perm):
    high = x.astype(jnp.bfloat16)
    rest = x - high.astype(jnp.float32)
    mid = rest.astype(jnp.bfloat16)
    low = (rest - mid.astype(jnp.float32)).astype(jnp.bfloat16)
    a, b, c = [jnp.dot(t, perm, preferred_element_type=jnp.float32) for t in (high, mid, low)]
    return (a + b) + c


def pieces(row):
    return [row[..., c : c + LANES] for c in range(0, row.shape[-1], LANES)]


def mapped(f, *args):
    return [f(*a) for a in zip(*args)]


def pair_modes(x, lane):
    n = from_next(x, lane)
    return mapped(lambda a, b: a + b, x, n), mapped(lambda a, b: b - a, x, n)


def element_modes(here, above):
    (p0, m0), (p1, m1) = here, above
    gx = mapped(lambda a, b: b - a, p0, p1)
    gy = mapped(lambda a, b: b + a, m0, m1)
    tw = mapped(lambda a, b: b - a, m0, m1)
    return gx, gy, tw


def pack_kernel(part, base, pat, both, own, lo, hi, perm, tmp):
    rows, cols = both.shape[0] // 2, both.shape[1]
    width = cols // LANES
    j = lax.broadcasted_iota(jnp.int32, (cols, LANES), 0)
    l = lax.broadcasted_iota(jnp.int32, (cols, LANES), 1)
    for c in range(width):
        one = jnp.where(j == width * l + c, 1.0, 0.0).astype(jnp.bfloat16)
        perm[:, c * LANES : (c + 1) * LANES] = one
    start, size = base * 2 * rows, part * 2 * rows
    for b in range(0, size, LANES):
        y = rearranged(pat[start + b : start + b + LANES, :], perm[...])
        for c, p in enumerate(pieces(y)):
            tmp[c, b : b + LANES, :] = p
    for k in range(2):
        for r in range(rows):
            for g in range(part // SUB):
                for c in range(width):
                    x = tmp[c, pl.ds((g * SUB * 2 + k) * rows + r, SUB, stride=2 * rows), :]
                    cs = slice(c * LANES, (c + 1) * LANES)
                    at = (k * rows + r) * part + g * SUB
                    own[at : at + SUB, cs] = x
                    if r >= rows - LO:
                        at = (k * LO + r - rows + LO) * part + g * SUB
                        lo[at : at + SUB, cs] = x
                    if r < HI:
                        at = (k * HI + r) * part + g * SUB
                        hi[at : at + SUB, cs] = x
    if base == 0:
        mixed = rearranged(both[...], perm[...])
        for i in range(2):
            field = mixed[i * rows : (i + 1) * rows]
            at = part * 2 * rows + i * rows
            own[at : at + rows, :] = field
            at = part * 2 * LO + i * LO
            lo[at : at + LO, :] = field[rows - LO :]
            at = part * 2 * HI + i * HI
            hi[at : at + HI, :] = field[:HI]


def krylov_kernel(groups, rows, base, count, own, lo, hi, own0, lo0, hi0, *rest):
    if base:
        before, rest = rest[0], rest[1:]
    else:
        dext, back, divisor, rest = *rest[2:5], rest[:2] + rest[5:]
    v, msg, ea, ec, eh, free, acc = rest
    cols = own.shape[1]
    total_rows = rows + LO + HI
    lane = lax.broadcasted_iota(jnp.int32, (SUB, LANES), 1)
    sublane = lax.broadcasted_iota(jnp.int32, (SUB, LANES), 0)
    part = groups * SUB
    lo_base, own_base = lo0.shape[0] - 2 * LO, own0.shape[0] - 2 * rows
    hi_base = hi0.shape[0] - 2 * HI

    for r in range(total_rows):
        if r < LO:
            d = lo0[lo_base + r : lo_base + r + 1, :]
            f = lo0[lo_base + LO + r : lo_base + LO + r + 1, :]
        elif r < LO + rows:
            k = own_base + r - LO
            d = own0[k : k + 1, :]
            f = own0[k + rows : k + rows + 1, :]
        else:
            k = r - LO - rows
            d = hi0[hi_base + k : hi_base + k + 1, :]
            f = hi0[hi_base + HI + k : hi_base + HI + k + 1, :]
        free[r] = jnp.broadcast_to(f, (SUB, cols))
        if not base:
            dext[r : r + 1, :] = d
        if r < total_rows - 1:
            y = jnp.where(d > 0.0, EMIN + d * d * d * (1.0 - EMIN), 0.0)
            y = jnp.broadcast_to(y, (SUB, cols))
            ea[r] = y * STRETCH
            ec[r] = y * SHEAR
            eh[r] = y * TWIST

    def group(g, _):
        at = pl.ds(pl.multiple_of(g * SUB, SUB), SUB)
        for r in range(total_rows):
            for k in range(2):
                if r < LO:
                    x = lo[pl.ds(pl.multiple_of((k * LO + r) * part + g * SUB, SUB), SUB), :]
                elif r < LO + rows:
                    x = own[pl.ds(pl.multiple_of((k * rows + r - LO) * part + g * SUB, SUB), SUB), :]
                else:
                    x = hi[pl.ds(pl.multiple_of((k * HI + r - LO - rows) * part + g * SUB, SUB), SUB), :]
                v[0, k, r, at, :] = x * free[r]

        sums = [None] * MOMENTS

        def add(i, a, b):
            for p, q in zip(a, b):
                sums[i] = p * q if sums[i] is None else sums[i] + p * q

        for it in range(ITERS):
            last = it == ITERS - 1
            first_e = LO if last else it
            last_e = LO + rows - 1 if last else total_rows - 2 - it
            here = [pair_modes(pieces(v[it, k, first_e, at, :]), lane) for k in range(2)]
            prior = None
            for e in range(first_e, last_e + 1):
                above = [pair_modes(pieces(v[it, k, e + 1, at, :]), lane) for k in range(2)]
                gxu, gyu, twu = element_modes(here[0], above[0])
                gxv, gyv, twv = element_modes(here[1], above[1])
                here = above
                a, c, h = pieces(ea[e]), pieces(ec[e]), pieces(eh[e])
                tx = mapped(lambda y, s, t: y * (s + NU * t), a, gxu, gyv)
                ty = mapped(lambda y, s, t: y * (NU * s + t), a, gxu, gyv)
                gs = mapped(lambda s, t: s + t, gyu, gxv)
                tg = mapped(lambda y, s: y * s, c, gs)
                hu = mapped(lambda y, s: y * s, h, twu)
                hv = mapped(lambda y, s: y * s, h, twv)
                if last:
                    for s, t in ((tx, gxu), (ty, gyv), (tg, gs), (hu, twu), (hv, twv)):
                        add(MOMENTS - 1, s, t)
                    continue
                up = [
                    (tx, mapped(lambda s, t: s + t, tg, hu)),
                    (tg, mapped(lambda s, t: s + t, ty, hv)),
                ]
                if prior is not None:
                    dn = [mapped(lambda s, t: s - t, tg, hu), mapped(lambda s, t: s - t, ty, hv)]
                    mask = pieces(free[e])
                    for k in range(2):
                        t = mapped(lambda s, t: s - t, prior[k][0], up[k][0])
                        q = mapped(lambda s, t: s + t, prior[k][1], dn[k])
                        left = mapped(lambda s, t: s - t, t, q)
                        right = from_prev(mapped(lambda s, t: s + t, t, q), lane)
                        out = mapped(lambda s, t, m: (s + t) * m, left, right, mask)
                        for c0, o in enumerate(out):
                            v[it + 1, k, e, at, c0 * LANES : (c0 + 1) * LANES] = o
                        if LO <= e < LO + rows:
                            src = pieces(v[it, k, e, at, :])
                            if it == 0:
                                add(0, src, src)
                            add(2 * it + 1, src, out)
                            add(2 * it + 2, out, out)
                prior = up
        for i in range(MOMENTS):
            acc[i, at, :] = sums[i]
        return 0

    lax.fori_loop(0, groups, group, 0)

    if not base:
        i = lax.broadcasted_iota(jnp.int32, (LANES, cols), 0)
        j = lax.broadcasted_iota(jnp.int32, (LANES, cols), 1)
        for c in range(cols // LANES):
            one = jnp.where(j == (cols // LANES) * i + c, 1.0, 0.0).astype(jnp.bfloat16)
            back[c * LANES : (c + 1) * LANES, :] = one
        inside = [
            pieces(jnp.where(dext[LO - 1 + i : LO - 1 + i + rows, :] > 0.0, 1.0, 0.0))
            for i in range(3)
        ]
        ones = taps(lane, *inside)
        own_d = pieces(dext[LO : LO + rows, :])
        divisor[...] = jnp.concatenate(mapped(lambda a, b: a * b, ones, own_d), 1)

    per = LANES // count
    for r in range(msg.shape[1]):
        row = jnp.zeros((SUB, LANES), jnp.float32)
        for i in range(r * per, (r + 1) * per):
            for g in range(groups):
                s = jnp.sum(acc[i, g * SUB : (g + 1) * SUB, :], axis=1, keepdims=True)
                first = (i - r * per) * count + base + g * SUB
                row = row + jnp.where(lane == sublane + first, s, 0.0)
        row = jnp.sum(row, axis=0, keepdims=True)
        row = row + before[0, r : r + 1, :] if base else row
        for t in range(msg.shape[0]):
            msg[t, r : r + 1, :] = row


def exact_sum(terms):
    pairs = [(t, jnp.zeros_like(t)) for t in terms]
    while len(pairs) > 1:
        merged = []
        for (a, e), (b, f) in zip(pairs[::2], pairs[1::2]):
            s = a + b
            v = s - a
            merged.append((s, ((a - (s - v)) + (b - v)) + (e + f)))
        pairs = merged + pairs[len(pairs) - len(pairs) % 2 :]
    return pairs[0][0] + pairs[0][1]


def coefficients(m):
    zero = jnp.zeros_like(m[0])
    s_prev, s = [zero] * MOMENTS, list(m)
    a, b = [m[1] / m[0]], [m[0]]
    fine = [m[0] > 0.0]
    for k in range(1, ITERS):
        n = [None] * MOMENTS
        for l in range(k, MOMENTS - k):
            n[l] = s[l + 1] - a[k - 1] * s[l]
            if k > 1:
                n[l] = n[l] - b[k - 1] * s_prev[l]
        scale = jnp.abs(s[k + 1]) + jnp.abs(a[k - 1] * s[k])
        fine.append(fine[-1] & (n[k] > 1e-6 * scale))
        a.append(n[k + 1] / n[k] - s[k] / s[k - 1])
        b.append(n[k] / s[k - 1])
        s_prev, s = s, n
    x = [zero] * ITERS
    r = [jnp.ones_like(zero)] + [zero] * (ITERS - 1)
    p = list(r)
    total = zero
    rr, d, good = m[0], a[0], fine[0] & (a[0] > 0.0)
    for k in range(ITERS):
        alpha = jnp.where(good, 1.0 / d, 0.0)
        total = total + jnp.where(good, alpha * rr, 0.0)
        for j in range(k + 1):
            x[j] = x[j] + jnp.where(good, alpha * p[j], 0.0)
        if k + 1 < ITERS:
            r = [r[j] - (alpha * p[j - 1] if j else 0.0) for j in range(ITERS)]
            ratio = b[k + 1] / (d * d)
            p = [r[j] + ratio * p[j] for j in range(ITERS)]
            rr = rr * ratio
            d = a[k + 1] - b[k + 1] / d
            good = good & fine[k + 1] & (d > 0.0)
    return x, total


def finish_kernel(count, elements, *refs):
    vs, refs = refs[:-9], refs[-9:]
    msgs, dext, back, divisor, cases, sens, comp, energy, rimmed = refs
    rows, cols = sens.shape
    lane = lax.broadcasted_iota(jnp.int32, (SUB, LANES), 1)
    sublane = lax.broadcasted_iota(jnp.int32, (SUB, LANES), 0)
    m = exact_sum([msgs[i] for i in range(msgs.shape[0])])
    per = LANES // count
    moments = []
    for i in range(MOMENTS):
        row = jnp.broadcast_to(m[i // per : i // per + 1, :], (SUB, LANES))
        shift = i % per * count
        moments.append(pltpu.roll(row, LANES - shift, 1) if shift else row)
    xs, total = coefficients(moments)
    real = lane < count
    total = jnp.where(real, total, 0.0)
    mean = jnp.sum(total, axis=1, keepdims=True) / count
    weight = 1.0 / count + 2.0 * KAPPA / count * (total - mean) / mean

    def by_case(row, g):
        s = jnp.where(lane == sublane + g * SUB, row, 0.0)
        return jnp.broadcast_to(jnp.sum(s, axis=1, keepdims=True), (SUB, LANES))

    picked = jnp.zeros((SUB, count), jnp.float32)
    for g in range(count // SUB):
        match = jnp.broadcast_to(cases[...], (SUB, count)) == sublane[:, :count] + g * SUB
        picked = picked + jnp.where(match, by_case(total, g)[:, :count], 0.0)
    comp[...] = jnp.sum(picked, axis=0, keepdims=True) / elements

    span = rows + 2
    first = True
    gi = -1
    for ref in vs:
        groups = ref.shape[3] // SUB
        for g in range(groups):
            gi += 1
            at = slice(g * SUB, (g + 1) * SUB)
            co = [by_case(x, gi) for x in xs]
            w = by_case(weight, gi)

            def node(r):
                out = []
                for k in range(2):
                    vals = [pieces(ref[j, k, r, at, :]) for j in range(ITERS)]
                    x = mapped(lambda *q: sum(c * s for c, s in zip(co[1:], q[1:])) + co[0] * q[0], *vals)
                    out.append(pair_modes(x, lane))
                return out

            here = node(LO - 1)
            for e in range(span):
                above = node(LO + e)
                gxu, gyu, twu = element_modes(here[0], above[0])
                gxv, gyv, twv = element_modes(here[1], above[1])
                here = above
                for c in range(cols // LANES):
                    sh = gyu[c] + gxv[c]
                    en = STRETCH * (gxu[c] * gxu[c] + gyv[c] * gyv[c] + (2.0 * NU) * (gxu[c] * gyv[c]))
                    en = en + SHEAR * (sh * sh) + TWIST * (twu[c] * twu[c] + twv[c] * twv[c])
                    en = w * en
                    cs = slice(c * LANES, (c + 1) * LANES)
                    energy[e, :, cs] = en if first else energy[e, :, cs] + en
            first = False

    for e in range(span):
        d = dext[LO - 1 + e : LO + e, :]
        s = jnp.sum(energy[e], axis=0, keepdims=True)
        rimmed[e : e + 1, :] = (-(elements / mean[:1]) * 3.0 * (1.0 - EMIN)) * (d * d * d * s)

    top = taps(lane, *[pieces(rimmed[i : i + rows, :]) for i in range(3)])
    out = jnp.concatenate(mapped(lambda a, b: a / b, top, pieces(divisor[...])), 1)
    sens[...] = rearranged(out, back[...])


def local(patterns, cases, density, supports):
    rows, cols = density.shape
    count = patterns.shape[0]
    tiles = lax.axis_size("space")
    parts = [count // SHARES] * SHARES
    total_rows = rows + LO + HI
    up = [(i, i + 1) for i in range(tiles - 1)]
    down = [(i + 1, i) for i in range(tiles - 1)]
    flat = patterns.reshape(count * 2 * rows, cols)
    vmem = pl.BlockSpec(memory_space=pltpu.VMEM)
    params = pltpu.CompilerParams(vmem_limit_bytes=12 * 2**20)

    def shape(*dims):
        return jax.ShapeDtypeStruct(dims, jnp.float32)

    fixed = jnp.pad(supports, ((rows, 0), (0, 0)), constant_values=1)
    both = jnp.pad(density, ((0, rows), (0, 0))) + (1 - fixed).astype(jnp.float32)
    owns, lows, highs = [], [], []
    for c, part in enumerate(parts):
        base = sum(parts[:c])
        extra = 0 if c else 2
        own, low, high = pl.pallas_call(
            functools.partial(pack_kernel, part, base),
            out_shape=tuple(shape(n * (2 * part + extra), cols) for n in (rows, LO, HI)),
            in_specs=[vmem] * 2,
            out_specs=(vmem,) * 3,
            scratch_shapes=[
                pltpu.VMEM((cols, cols), jnp.bfloat16),
                pltpu.VMEM((cols // LANES, part * 2 * rows, LANES), jnp.float32),
            ],
            compiler_params=params,
            name="pack",
        )(flat, both)
        owns.append(own)
        lows.append(lax.ppermute(low, "space", up))
        highs.append(lax.ppermute(high, "space", down))

    vs, msg, extras = [], None, None
    for c, part in enumerate(parts):
        args = (owns[c], lows[c], highs[c], owns[0], lows[0], highs[0]) + ((msg,) if c else ())
        outs = (
            shape(ITERS, 2, total_rows, part, cols),
            shape(tiles if c + 1 == len(parts) else 1, MOMENTS * count // LANES, LANES),
        )
        if not c:
            outs += (
                shape(total_rows, cols),
                jax.ShapeDtypeStruct((cols, cols), jnp.bfloat16),
                shape(rows, cols),
            )
        v, msg, *more = pl.pallas_call(
            functools.partial(krylov_kernel, part // SUB, rows, sum(parts[:c]), count),
            out_shape=outs,
            in_specs=[vmem] * len(args),
            out_specs=(vmem,) * len(outs),
            scratch_shapes=[
                pltpu.VMEM((total_rows - 1, SUB, cols), jnp.float32),
                pltpu.VMEM((total_rows - 1, SUB, cols), jnp.float32),
                pltpu.VMEM((total_rows - 1, SUB, cols), jnp.float32),
                pltpu.VMEM((total_rows, SUB, cols), jnp.float32),
                pltpu.VMEM((MOMENTS, part, LANES), jnp.float32),
            ],
            compiler_params=params,
            cost_estimate=pl.CostEstimate(flops=10**10, bytes_accessed=40 * 10**6, transcendentals=0),
            name="krylov",
        )(*args)
        vs.append(v)
        extras = extras if c else more

    msgs = lax.all_to_all(msg, "space", 0, 0)
    sens, comp = pl.pallas_call(
        functools.partial(finish_kernel, count, rows * tiles * cols),
        out_shape=(shape(rows, cols), shape(1, count)),
        in_specs=[vmem] * (len(vs) + 5),
        out_specs=(vmem,) * 2,
        scratch_shapes=[
            pltpu.VMEM((rows + 2, SUB, cols), jnp.float32),
            pltpu.VMEM((rows + SUB, cols), jnp.float32),
        ],
        compiler_params=params,
        name="finish",
    )(*vs, msgs, *extras, cases[None])
    return sens, comp.reshape(count)


def solution(mesh):
    in_specs = (
        P("groups", None, "space", None),
        P("groups"),
        P(("groups", "space"), None),
        P(("groups", "space"), None),
    )
    out_specs = (P(("groups", "space"), None), P("groups"))
    return jax.shard_map(local, mesh=mesh, in_specs=in_specs, out_specs=out_specs, check_vma=False)
```

```python
import functools

import jax
import jax.numpy as jnp
from jax import lax
from jax.experimental import pallas as pl
from jax.experimental.pallas import tpu as pltpu
from jax.sharding import PartitionSpec as P

ITERS = 4
EMIN = 0.001
KAPPA = 1.0
NU = 0.3
CENTRE = 1.5
EDGE = 0.5
CORNER = 1.5 - 2.0**0.5

LO = ITERS
HI = ITERS + 1
MOMENTS = 2 * ITERS

STRETCH = 1.0 / (4.0 * (1.0 - NU * NU))
SHEAR = 1.0 / (8.0 * (1.0 + NU))
TWIST = (3.0 - NU) / (24.0 * (1.0 - NU * NU))

LANES = 128
SUB = 8
SHARES = 2


def from_next(x, lane):
    r = pltpu.roll(x[0], LANES - 1, 1)
    return x[1:] + [jnp.where(lane == LANES - 1, 0.0, r)]


def from_prev(x, lane):
    r = pltpu.roll(x[-1], 1, 1)
    return [jnp.where(lane == 0, 0.0, r)] + x[:-1]


def taps(lane, up, mid, dn):
    side = mapped(lambda a, b: a + b, up, dn)
    total = mapped(lambda a, b: CENTRE * a + EDGE * b, mid, side)
    sides = mapped(lambda a, b: EDGE * a + CORNER * b, mid, side)
    left, right = from_prev(sides, lane), from_next(sides, lane)
    return mapped(lambda a, b, c: a + b + c, total, left, right)


def rearranged(x, perm):
    high = x.astype(jnp.bfloat16)
    rest = x - high.astype(jnp.float32)
    mid = rest.astype(jnp.bfloat16)
    low = (rest - mid.astype(jnp.float32)).astype(jnp.bfloat16)
    a, b, c = [jnp.dot(t, perm, preferred_element_type=jnp.float32) for t in (high, mid, low)]
    return (a + b) + c


def pieces(row):
    return [row[..., c : c + LANES] for c in range(0, row.shape[-1], LANES)]


def mapped(f, *args):
    return [f(*a) for a in zip(*args)]


def pair_modes(x, lane):
    n = from_next(x, lane)
    return mapped(lambda a, b: a + b, x, n), mapped(lambda a, b: b - a, x, n)


def element_modes(here, above):
    (p0, m0), (p1, m1) = here, above
    gx = mapped(lambda a, b: b - a, p0, p1)
    gy = mapped(lambda a, b: b + a, m0, m1)
    tw = mapped(lambda a, b: b - a, m0, m1)
    return gx, gy, tw


def pack_kernel(part, base, pat, both, own, lo, hi, perm, tmp):
    rows, cols = both.shape[0] // 2, both.shape[1]
    width = cols // LANES
    j = lax.broadcasted_iota(jnp.int32, (cols, LANES), 0)
    l = lax.broadcasted_iota(jnp.int32, (cols, LANES), 1)
    for c in range(width):
        one = jnp.where(j == width * l + c, 1.0, 0.0).astype(jnp.bfloat16)
        perm[:, c * LANES : (c + 1) * LANES] = one
    start, size = base * 2 * rows, part * 2 * rows
    for b in range(0, size, LANES):
        y = rearranged(pat[start + b : start + b + LANES, :], perm[...])
        for c, p in enumerate(pieces(y)):
            tmp[c, b : b + LANES, :] = p
    for k in range(2):
        for r in range(rows):
            for g in range(part // SUB):
                for c in range(width):
                    x = tmp[c, pl.ds((g * SUB * 2 + k) * rows + r, SUB, stride=2 * rows), :]
                    cs = slice(c * LANES, (c + 1) * LANES)
                    at = (k * rows + r) * part + g * SUB
                    own[at : at + SUB, cs] = x
                    if r >= rows - LO:
                        at = (k * LO + r - rows + LO) * part + g * SUB
                        lo[at : at + SUB, cs] = x
                    if r < HI:
                        at = (k * HI + r) * part + g * SUB
                        hi[at : at + SUB, cs] = x
    if base == 0:
        mixed = rearranged(both[...], perm[...])
        for i in range(2):
            field = mixed[i * rows : (i + 1) * rows]
            at = part * 2 * rows + i * rows
            own[at : at + rows, :] = field
            at = part * 2 * LO + i * LO
            lo[at : at + LO, :] = field[rows - LO :]
            at = part * 2 * HI + i * HI
            hi[at : at + HI, :] = field[:HI]


def sweeps(stage, it, rows):
    end = rows + LO + HI - 2
    if it == ITERS - 1:
        runs = {
            "all": [(LO, LO + rows - 1)],
            "inner": [(LO + it, LO + rows - 2 - it)],
            "outer": [(LO, LO + it - 1), (LO + rows - 1 - it, LO + rows - 1)],
        }
    else:
        runs = {
            "all": [(it, end - it)],
            "inner": [(LO + it, LO + rows - 2 - it)],
            "outer": [(it, LO + it), (LO + rows - 2 - it, end - it)],
        }
    return runs[stage]


def krylov_kernel(groups, rows, base, count, stage, *refs):
    if stage == "inner":
        own, ea, ec, eh, free, v, acc = refs
    elif stage == "outer":
        lo, hi, ea, ec, eh, free, before, _, start, v, msg, acc = refs
    else:
        own, lo, hi, v, msg, ea, ec, eh, free, dext, back, divisor, acc = refs
    part = groups * SUB
    cols = v.shape[-1]
    total_rows = rows + LO + HI
    lane = lax.broadcasted_iota(jnp.int32, (SUB, LANES), 1)
    sublane = lax.broadcasted_iota(jnp.int32, (SUB, LANES), 0)
    part = groups * SUB
    lo_base, own_base, hi_base = part * 2 * LO, part * 2 * rows, part * 2 * HI

    for r in range(total_rows if stage == "all" else 0):
        if r < LO:
            d = lo[lo_base + r : lo_base + r + 1, :]
            f = lo[lo_base + LO + r : lo_base + LO + r + 1, :]
        elif r < LO + rows:
            k = own_base + r - LO
            d = own[k : k + 1, :]
            f = own[k + rows : k + rows + 1, :]
        else:
            k = r - LO - rows
            d = hi[hi_base + k : hi_base + k + 1, :]
            f = hi[hi_base + HI + k : hi_base + HI + k + 1, :]
        free[r] = jnp.broadcast_to(f, (SUB, cols))
        dext[r : r + 1, :] = d
        if r < total_rows - 1:
            y = jnp.where(d > 0.0, EMIN + d * d * d * (1.0 - EMIN), 0.0)
            y = jnp.broadcast_to(y, (SUB, cols))
            ea[r] = y * STRETCH
            ec[r] = y * SHEAR
            eh[r] = y * TWIST

    def group(g, _):
        at = pl.ds(pl.multiple_of(g * SUB, SUB), SUB)
        for r in range(total_rows):
            if stage == ("outer" if LO <= r < LO + rows else "inner"):
                continue
            for k in range(2):
                if r < LO:
                    x = lo[pl.ds(pl.multiple_of((k * LO + r) * part + g * SUB, SUB), SUB), :]
                elif r < LO + rows:
                    x = own[pl.ds(pl.multiple_of((k * rows + r - LO) * part + g * SUB, SUB), SUB), :]
                else:
                    x = hi[pl.ds(pl.multiple_of((k * HI + r - LO - rows) * part + g * SUB, SUB), SUB), :]
                v[0, k, r, at, :] = x * free[r]

        sums = [start[i, at, :] if stage == "outer" else None for i in range(MOMENTS)]

        def add(i, a, b):
            for p, q in zip(a, b):
                sums[i] = p * q if sums[i] is None else sums[i] + p * q

        for it in range(ITERS):
            last = it == ITERS - 1
            for first_e, last_e in sweeps(stage, it, rows):
                here = [pair_modes(pieces(v[it, k, first_e, at, :]), lane) for k in range(2)]
                prior = None
                for e in range(first_e, last_e + 1):
                    above = [pair_modes(pieces(v[it, k, e + 1, at, :]), lane) for k in range(2)]
                    gxu, gyu, twu = element_modes(here[0], above[0])
                    gxv, gyv, twv = element_modes(here[1], above[1])
                    here = above
                    a, c, h = pieces(ea[e]), pieces(ec[e]), pieces(eh[e])
                    tx = mapped(lambda y, s, t: y * (s + NU * t), a, gxu, gyv)
                    ty = mapped(lambda y, s, t: y * (NU * s + t), a, gxu, gyv)
                    gs = mapped(lambda s, t: s + t, gyu, gxv)
                    tg = mapped(lambda y, s: y * s, c, gs)
                    hu = mapped(lambda y, s: y * s, h, twu)
                    hv = mapped(lambda y, s: y * s, h, twv)
                    if last:
                        for s, t in ((tx, gxu), (ty, gyv), (tg, gs), (hu, twu), (hv, twv)):
                            add(MOMENTS - 1, s, t)
                        continue
                    up = [
                        (tx, mapped(lambda s, t: s + t, tg, hu)),
                        (tg, mapped(lambda s, t: s + t, ty, hv)),
                    ]
                    if prior is not None:
                        dn = [mapped(lambda s, t: s - t, tg, hu), mapped(lambda s, t: s - t, ty, hv)]
                        mask = pieces(free[e])
                        for k in range(2):
                            t = mapped(lambda s, t: s - t, prior[k][0], up[k][0])
                            q = mapped(lambda s, t: s + t, prior[k][1], dn[k])
                            left = mapped(lambda s, t: s - t, t, q)
                            right = from_prev(mapped(lambda s, t: s + t, t, q), lane)
                            out = mapped(lambda s, t, m: (s + t) * m, left, right, mask)
                            for c0, o in enumerate(out):
                                v[it + 1, k, e, at, c0 * LANES : (c0 + 1) * LANES] = o
                            if LO <= e < LO + rows:
                                src = pieces(v[it, k, e, at, :])
                                if it == 0:
                                    add(0, src, src)
                                add(2 * it + 1, src, out)
                                add(2 * it + 2, out, out)
                    prior = up
        for i in range(MOMENTS):
            acc[i, at, :] = sums[i]
        return 0

    lax.fori_loop(0, groups, group, 0)

    if stage == "inner":
        return
    if stage == "all":
        i = lax.broadcasted_iota(jnp.int32, (LANES, cols), 0)
        j = lax.broadcasted_iota(jnp.int32, (LANES, cols), 1)
        for c in range(cols // LANES):
            one = jnp.where(j == (cols // LANES) * i + c, 1.0, 0.0).astype(jnp.bfloat16)
            back[c * LANES : (c + 1) * LANES, :] = one
        inside = [
            pieces(jnp.where(dext[LO - 1 + i : LO - 1 + i + rows, :] > 0.0, 1.0, 0.0))
            for i in range(3)
        ]
        ones = taps(lane, *inside)
        own_d = pieces(dext[LO : LO + rows, :])
        divisor[...] = jnp.concatenate(mapped(lambda a, b: a * b, ones, own_d), 1)

    per = LANES // count
    for r in range(msg.shape[1]):
        row = jnp.zeros((SUB, LANES), jnp.float32)
        for i in range(r * per, (r + 1) * per):
            for g in range(groups):
                s = jnp.sum(acc[i, g * SUB : (g + 1) * SUB, :], axis=1, keepdims=True)
                first = (i - r * per) * count + base + g * SUB
                row = row + jnp.where(lane == sublane + first, s, 0.0)
        row = jnp.sum(row, axis=0, keepdims=True)
        row = row + before[0, r : r + 1, :] if base else row
        for t in range(msg.shape[0]):
            msg[t, r : r + 1, :] = row


def exact_sum(terms):
    pairs = [(t, jnp.zeros_like(t)) for t in terms]
    while len(pairs) > 1:
        merged = []
        for (a, e), (b, f) in zip(pairs[::2], pairs[1::2]):
            s = a + b
            v = s - a
            merged.append((s, ((a - (s - v)) + (b - v)) + (e + f)))
        pairs = merged + pairs[len(pairs) - len(pairs) % 2 :]
    return pairs[0][0] + pairs[0][1]


def coefficients(m):
    zero = jnp.zeros_like(m[0])
    s_prev, s = [zero] * MOMENTS, list(m)
    a, b = [m[1] / m[0]], [m[0]]
    fine = [m[0] > 0.0]
    for k in range(1, ITERS):
        n = [None] * MOMENTS
        for l in range(k, MOMENTS - k):
            n[l] = s[l + 1] - a[k - 1] * s[l]
            if k > 1:
                n[l] = n[l] - b[k - 1] * s_prev[l]
        scale = jnp.abs(s[k + 1]) + jnp.abs(a[k - 1] * s[k])
        fine.append(fine[-1] & (n[k] > 1e-6 * scale))
        a.append(n[k + 1] / n[k] - s[k] / s[k - 1])
        b.append(n[k] / s[k - 1])
        s_prev, s = s, n
    x = [zero] * ITERS
    r = [jnp.ones_like(zero)] + [zero] * (ITERS - 1)
    p = list(r)
    total = zero
    rr, d, good = m[0], a[0], fine[0] & (a[0] > 0.0)
    for k in range(ITERS):
        alpha = jnp.where(good, 1.0 / d, 0.0)
        total = total + jnp.where(good, alpha * rr, 0.0)
        for j in range(k + 1):
            x[j] = x[j] + jnp.where(good, alpha * p[j], 0.0)
        if k + 1 < ITERS:
            r = [r[j] - (alpha * p[j - 1] if j else 0.0) for j in range(ITERS)]
            ratio = b[k + 1] / (d * d)
            p = [r[j] + ratio * p[j] for j in range(ITERS)]
            rr = rr * ratio
            d = a[k + 1] - b[k + 1] / d
            good = good & fine[k + 1] & (d > 0.0)
    return x, total


def finish_kernel(count, elements, *refs):
    vs, refs = refs[:-9], refs[-9:]
    msgs, dext, back, divisor, cases, sens, comp, energy, rimmed = refs
    rows, cols = sens.shape
    lane = lax.broadcasted_iota(jnp.int32, (SUB, LANES), 1)
    sublane = lax.broadcasted_iota(jnp.int32, (SUB, LANES), 0)
    m = exact_sum([msgs[i] for i in range(msgs.shape[0])])
    per = LANES // count
    moments = []
    for i in range(MOMENTS):
        row = jnp.broadcast_to(m[i // per : i // per + 1, :], (SUB, LANES))
        shift = i % per * count
        moments.append(pltpu.roll(row, LANES - shift, 1) if shift else row)
    xs, total = coefficients(moments)
    real = lane < count
    total = jnp.where(real, total, 0.0)
    mean = jnp.sum(total, axis=1, keepdims=True) / count
    weight = 1.0 / count + 2.0 * KAPPA / count * (total - mean) / mean

    def by_case(row, g):
        s = jnp.where(lane == sublane + g * SUB, row, 0.0)
        return jnp.broadcast_to(jnp.sum(s, axis=1, keepdims=True), (SUB, LANES))

    picked = jnp.zeros((SUB, count), jnp.float32)
    for g in range(count // SUB):
        match = jnp.broadcast_to(cases[...], (SUB, count)) == sublane[:, :count] + g * SUB
        picked = picked + jnp.where(match, by_case(total, g)[:, :count], 0.0)
    comp[...] = jnp.sum(picked, axis=0, keepdims=True) / elements

    span = rows + 2
    first = True
    gi = -1
    for ref in vs:
        groups = ref.shape[3] // SUB
        for g in range(groups):
            gi += 1
            at = slice(g * SUB, (g + 1) * SUB)
            co = [by_case(x, gi) for x in xs]
            w = by_case(weight, gi)

            def node(r):
                out = []
                for k in range(2):
                    vals = [pieces(ref[j, k, r, at, :]) for j in range(ITERS)]
                    x = mapped(lambda *q: sum(c * s for c, s in zip(co[1:], q[1:])) + co[0] * q[0], *vals)
                    out.append(pair_modes(x, lane))
                return out

            here = node(LO - 1)
            for e in range(span):
                above = node(LO + e)
                gxu, gyu, twu = element_modes(here[0], above[0])
                gxv, gyv, twv = element_modes(here[1], above[1])
                here = above
                for c in range(cols // LANES):
                    sh = gyu[c] + gxv[c]
                    en = STRETCH * (gxu[c] * gxu[c] + gyv[c] * gyv[c] + (2.0 * NU) * (gxu[c] * gyv[c]))
                    en = en + SHEAR * (sh * sh) + TWIST * (twu[c] * twu[c] + twv[c] * twv[c])
                    en = w * en
                    cs = slice(c * LANES, (c + 1) * LANES)
                    energy[e, :, cs] = en if first else energy[e, :, cs] + en
            first = False

    for e in range(span):
        d = dext[LO - 1 + e : LO + e, :]
        s = jnp.sum(energy[e], axis=0, keepdims=True)
        rimmed[e : e + 1, :] = (-(elements / mean[:1]) * 3.0 * (1.0 - EMIN)) * (d * d * d * s)

    top = taps(lane, *[pieces(rimmed[i : i + rows, :]) for i in range(3)])
    out = jnp.concatenate(mapped(lambda a, b: a / b, top, pieces(divisor[...])), 1)
    sens[...] = rearranged(out, back[...])


def local(patterns, cases, density, supports):
    rows, cols = density.shape
    count = patterns.shape[0]
    tiles = lax.axis_size("space")
    parts = [count // SHARES] * SHARES
    total_rows = rows + LO + HI
    up = [(i, i + 1) for i in range(tiles - 1)]
    down = [(i + 1, i) for i in range(tiles - 1)]
    flat = patterns.reshape(count * 2 * rows, cols)
    vmem = pl.BlockSpec(memory_space=pltpu.VMEM)
    params = pltpu.CompilerParams(vmem_limit_bytes=12 * 2**20)

    def shape(*dims):
        return jax.ShapeDtypeStruct(dims, jnp.float32)

    fixed = jnp.pad(supports, ((rows, 0), (0, 0)), constant_values=1)
    both = jnp.pad(density, ((0, rows), (0, 0))) + (1 - fixed).astype(jnp.float32)
    owns, lows, highs = [], [], []
    for c, part in enumerate(parts):
        base = sum(parts[:c])
        extra = 0 if c else 2
        own, low, high = pl.pallas_call(
            functools.partial(pack_kernel, part, base),
            out_shape=tuple(shape(n * (2 * part + extra), cols) for n in (rows, LO, HI)),
            in_specs=[vmem] * 2,
            out_specs=(vmem,) * 3,
            scratch_shapes=[
                pltpu.VMEM((cols, cols), jnp.bfloat16),
                pltpu.VMEM((cols // LANES, part * 2 * rows, LANES), jnp.float32),
            ],
            compiler_params=params,
            name="pack",
        )(flat, both)
        owns.append(own)
        lows.append(lax.ppermute(low, "space", up))
        highs.append(lax.ppermute(high, "space", down))

    vs, msg, fields, extras = [], None, (), ()
    def krylov(c, stage, args, outs, **options):
        part = parts[c]
        return pl.pallas_call(
            functools.partial(krylov_kernel, part // SUB, rows, sum(parts[:c]), count, stage),
            out_shape=outs,
            in_specs=[vmem] * len(args),
            out_specs=(vmem,) * len(outs),
            compiler_params=params,
            cost_estimate=pl.CostEstimate(
                flops=10**10, bytes_accessed=40 * 10**6, transcendentals=0
            ),
            name="krylov",
            **options,
        )(*args)

    for c, part in enumerate(parts):
        vectors = shape(ITERS, 2, total_rows, part, cols)
        sums = shape(MOMENTS, part, LANES)
        sends = tiles if c + 1 == len(parts) else 1
        message = shape(sends, MOMENTS * count // LANES, LANES)
        scratch = [pltpu.VMEM(sums.shape, jnp.float32)]
        if c:
            v, start = krylov(c, "inner", (owns[c], *fields), (vectors, sums))
            v, msg = krylov(
                c,
                "outer",
                (lows[c], highs[c], *fields, msg, v, start),
                (vectors, message),
                scratch_shapes=scratch,
                input_output_aliases={7: 0},
            )
        else:
            outs = (vectors, message) + (shape(total_rows - 1, SUB, cols),) * 3
            outs += (shape(total_rows, SUB, cols), shape(total_rows, cols))
            outs += (jax.ShapeDtypeStruct((cols, cols), jnp.bfloat16), shape(rows, cols))
            args = (owns[c], lows[c], highs[c])
            v, msg, *more = krylov(c, "all", args, outs, scratch_shapes=scratch)
            fields, extras = more[:4], more[4:]
        vs.append(v)

    msgs = lax.all_to_all(msg, "space", 0, 0)
    sens, comp = pl.pallas_call(
        functools.partial(finish_kernel, count, rows * tiles * cols),
        out_shape=(shape(rows, cols), shape(1, count)),
        in_specs=[vmem] * (len(vs) + 5),
        out_specs=(vmem,) * 2,
        scratch_shapes=[
            pltpu.VMEM((rows + 2, SUB, cols), jnp.float32),
            pltpu.VMEM((rows + SUB, cols), jnp.float32),
        ],
        compiler_params=params,
        name="finish",
    )(*vs, msgs, *extras, cases[None])
    return sens, comp.reshape(count)


def solution(mesh):
    in_specs = (
        P("groups", None, "space", None),
        P("groups"),
        P(("groups", "space"), None),
        P(("groups", "space"), None),
    )
    out_specs = (P(("groups", "space"), None), P("groups"))
    return jax.shard_map(local, mesh=mesh, in_specs=in_specs, out_specs=out_specs, check_vma=False)
```
